512 devices in a mesh: tm: 64 (over x_lo, z, core), tensor: 8 (over y, x_hi).
Axes of the slice: x: 4 (x_hi: 2, x_lo: 2; x = x_hi * 2 + x_lo), y: 4, z: 16, core: 2. Of those that a mesh axis runs over, the one named last changes fastest.
Arguments:
- tokens: bfloat16 [28672, 5120], P('tm'), may hold values from -64 to 64
- shift_mod: float32 [5120], replicated, may hold values from -3 to 3
- scale_mod: float32 [5120], replicated, may hold values from -3 to 3
- w_query: bfloat16 [5120, 3072], P('tm', 'tensor'), may hold values from -2 to 2
- w_key: bfloat16 [5120, 3072], P('tm', 'tensor'), may hold values from -2 to 2
- w_value: bfloat16 [5120, 3072], P('tm', 'tensor'), may hold values from -0.078125 to 0.078125
- prune_masks: int32 [3, 40, 24], P(None, None, 'tensor'), may hold values 0 or 1
- query_gain: float32 [3072], P('tensor'), may hold values from 1 to 2.5
- key_gain: float32 [3072], P('tensor'), may hold values from 1 to 2.5
Outputs:
- attended: bfloat16 [28672, 3072], P('tm', 'tensor')
The draws below stay inside these ranges and needn't reach their ends.
All inputs are finite; a program needn't handle non-finite values. No bound on the sum of `prune_masks` on one device may be relied on, other than what follows from the above.
Results may differ from the reference program's by a relative error of at most 0.012.
Values may be sent and summed in bfloat16 or wider, within the bound.
No kernel may reach another device: no remote copies, remote signals or barrier semaphores. Data moves between devices by JAX's collectives and lax.ppermute only.
A program may use at most 128 MiB of HBM per device.

```python
import math
import jax
import jax.numpy as jnp
from jax import lax

D = 5120
HEADS = 24
HD = 128
BLK = 128
TOK_FRAME = 448
FRAMES = 64
TOKENS = 28672


def shared_normal(key):
    return jax.random.normal(key, (D, HEADS * HD), jnp.float32)


def column_scales(key):
    head_of = (jnp.arange(HEADS * HD, dtype=jnp.int32) // HD).astype(jnp.float32)
    ramp = jnp.exp(0.5 * math.log(3.0) * head_of / max(HEADS - 1, 1))
    spread = jnp.exp(jax.random.uniform(key, (HEADS * HD,), jnp.float32, 0.0, math.log(10.0)))
    return ramp * spread / (3.0 * math.sqrt(D))


def draw_w_query(key, part):
    common = shared_normal(key)
    key = jax.random.fold_in(key, 1)
    values = common * column_scales(jax.random.fold_in(key, 2))[None, :]
    return jnp.clip(values, -2.0, 2.0).astype(jnp.bfloat16)


def draw_w_key(key, part):
    key = jax.random.fold_in(key, 3)
    own_normal = jax.random.normal(jax.random.fold_in(key, 1), (D, HEADS * HD), jnp.float32)
    values = own_normal * column_scales(jax.random.fold_in(key, 2))[None, :]
    return jnp.clip(values, -2.0, 2.0).astype(jnp.bfloat16)


def draw_tokens(key, part):
    key = jax.random.fold_in(key, 4)
    fresh = jax.random.normal(jax.random.fold_in(key, 1), (TOKENS, D), jnp.float32)
    return jnp.clip(fresh, -64.0, 64.0).astype(jnp.bfloat16)


def with_ends(drawn, key, smallest, largest):
    longest = drawn.shape.index(max(drawn.shape))
    spots = []
    for shift in (0, 1):
        where = [jax.random.randint(jax.random.fold_in(key, axis), (), 0, length) for axis, length in enumerate(drawn.shape)]
        where[longest] = (where[longest] + shift) % drawn.shape[longest]
        spots.append(tuple(where))
    return drawn.at[spots[0]].set(smallest).at[spots[1]].set(largest)


def block_levels(rng, extent, shards, least, largest):
    def one(axis_at, blocks):
        draws = jax.random.uniform(jax.random.fold_in(jax.random.fold_in(rng, 6), axis_at), (blocks,), jnp.float32, least / len(shards), largest / len(shards))
        return jnp.repeat(jnp.exp(draws), extent[axis_at] // blocks).reshape((-1,) + (1,) * (len(extent) - axis_at - 1))

    factor_of = one(*shards[0])
    for cut in shards[1:]:
        factor_of = factor_of * one(*cut)
    return factor_of


def noise(rng, extent, scale, limit, shards=(), held_as=jnp.bfloat16):
    drawn = jax.random.normal(rng, extent, jnp.float32) * scale
    if len(shards) > 0:
        drawn = block_levels(rng, extent, shards, -0.22, 0.18) * drawn
    return jnp.clip(drawn, min=-limit, max=limit).astype(held_as)


def setup_inputs(seed: int = 0) -> dict:
    streams_of = jax.random.split(jax.random.key(seed), 10)
    return {
        "tokens": draw_tokens(jax.random.fold_in(streams_of[9], 71), 0),
        "shift_mod": noise(streams_of[1], (D,), 0.5, 3.0, (), jnp.float32),
        "scale_mod": noise(streams_of[2], (D,), 0.5, 3.0, (), jnp.float32),
        "w_query": draw_w_query(jax.random.fold_in(streams_of[9], 71), 0),
        "w_key": draw_w_key(jax.random.fold_in(streams_of[9], 71), 0),
        "w_value": noise(streams_of[5], (D, HEADS * HD), D ** -0.5, 0.078125, ((0, 64), (1, 8))),
        "prune_masks": with_ends((jax.random.randint(streams_of[6], (3, D // BLK, HEADS * HD // BLK), 0, 4) < 3).astype(jnp.int32), jax.random.fold_in(streams_of[6], 1), 0, 1),
        "query_gain": jnp.clip(1.0 + 1.5 * jax.random.uniform(streams_of[7], (HEADS * HD,), jnp.float32) ** block_levels(streams_of[7], (HEADS * HD,), ((0, 8),), -0.2, 0.2), 1.0, 2.5),
        "key_gain": jnp.clip(1.0 + 1.5 * jax.random.uniform(streams_of[8], (HEADS * HD,), jnp.float32) ** block_levels(streams_of[8], (HEADS * HD,), ((0, 8),), -0.2, 0.2), 1.0, 2.5),
    }


eps_layer = 1e-06
eps_rms = 1e-06
neg_large = -1e+30

def modulate(tokens, shift_mod, scale_mod):
    values = tokens.astype(jnp.float32)
    average = lax.optimization_barrier(jnp.mean(values, axis=1, keepdims=True))
    centred = values - average
    variance = lax.optimization_barrier(jnp.mean(centred * centred, axis=1, keepdims=True))
    normalized = centred * lax.rsqrt(variance + eps_layer)
    return (normalized * (1.0 + scale_mod) + shift_mod).astype(jnp.bfloat16)

def rms_rows(raw_rows, gain):
    mean_square = lax.optimization_barrier(jnp.mean(raw_rows * raw_rows, axis=1, keepdims=True))
    return (raw_rows * lax.rsqrt(mean_square + eps_rms) * gain).astype(jnp.bfloat16)

def reference(tokens, shift_mod, scale_mod, w_query, w_key, w_value, prune_masks, query_gain, key_gain):
    normed = modulate(tokens, shift_mod, scale_mod)
    kept = jnp.repeat(jnp.repeat(prune_masks, BLK, axis=1), BLK, axis=2).astype(jnp.bfloat16)
    query_raw = jnp.dot(normed, w_query * kept[0], preferred_element_type=jnp.float32)
    key_raw = jnp.dot(normed, w_key * kept[1], preferred_element_type=jnp.float32)
    value_raw = jnp.dot(normed, w_value * kept[2], preferred_element_type=jnp.float32)
    query_rows = rms_rows(query_raw, query_gain)
    key_rows = rms_rows(key_raw, key_gain)
    value_rows = value_raw.astype(jnp.bfloat16)
    width = HEADS * HD
    padding = jnp.zeros((2 * TOK_FRAME, width), jnp.bfloat16)
    keys_padded = jnp.concatenate([padding, key_rows], axis=0)
    values_padded = jnp.concatenate([padding, value_rows], axis=0)

    def one_frame(frame):
        first_row = (frame * TOK_FRAME).astype(jnp.int32)
        query_block = lax.dynamic_slice_in_dim(query_rows, first_row, TOK_FRAME, 0)
        key_block = lax.dynamic_slice_in_dim(keys_padded, first_row, 3 * TOK_FRAME, 0)
        value_block = lax.dynamic_slice_in_dim(values_padded, first_row, 3 * TOK_FRAME, 0)
        query_heads = query_block.reshape(TOK_FRAME, HEADS, HD).astype(jnp.float32)
        key_heads = key_block.reshape(3 * TOK_FRAME, HEADS, HD).astype(jnp.float32)
        value_heads = value_block.reshape(3 * TOK_FRAME, HEADS, HD).astype(jnp.float32)
        score = jnp.einsum('qhd,khd->hqk', query_heads, key_heads) * HD ** (-0.5)
        key_frame = frame - 2 + jnp.arange(3 * TOK_FRAME, dtype=jnp.int32) // TOK_FRAME
        allowed = key_frame >= 0
        score = jnp.where(allowed[None, None, :], score, neg_large)
        row_max = lax.optimization_barrier(jnp.max(score, axis=2, keepdims=True))
        exponent = jnp.exp(score - row_max)
        probs = (exponent / lax.optimization_barrier(jnp.sum(exponent, axis=2, keepdims=True))).astype(jnp.bfloat16)
        mixed = jnp.einsum('hqk,khd->qhd', probs.astype(jnp.float32), value_heads)
        return mixed.reshape(TOK_FRAME, width).astype(jnp.bfloat16)
    frames_out = lax.map(one_frame, jnp.arange(FRAMES, dtype=jnp.int32))
    return frames_out.reshape(TOKENS, width)
```

```python
import jax
import jax.numpy as jnp
from jax import lax
from jax.experimental import pallas as pl
from jax.experimental.pallas import tpu as pltpu
from jax.sharding import PartitionSpec as P

HEADS = 24
HD = 128
BLK = 128
LOG2E = 1.4426950408889634

eps_layer = 1e-06
eps_rms = 1e-06
neg_large = -1e30
VMEM = pltpu.CompilerParams(vmem_limit_bytes=56 * 1024 * 1024)


def grid_of(mesh):
    return 2, mesh.shape["tm"] // 4, 2


def norm_kernel(tok_ref, shift_ref, scale_ref, out_ref):
    values = tok_ref[...].astype(jnp.float32)
    width = values.shape[1]
    average = jnp.sum(values, axis=1, keepdims=True) * (1.0 / width)
    centred = values - average
    variance = jnp.sum(centred * centred, axis=1, keepdims=True) * (1.0 / width)
    normalized = centred * lax.rsqrt(variance + eps_layer)
    out_ref[...] = (normalized * (1.0 + scale_ref[...]) + shift_ref[...]).astype(jnp.bfloat16)


def modulate(tokens, shift_mod, scale_mod):
    rows, width = tokens.shape
    step = 64
    return pl.pallas_call(
        norm_kernel,
        grid=(rows // step,),
        in_specs=[
            pl.BlockSpec((step, width), lambda i: (i, 0)),
            pl.BlockSpec((1, width), lambda i: (0, 0)),
            pl.BlockSpec((1, width), lambda i: (0, 0)),
        ],
        out_specs=pl.BlockSpec((step, width), lambda i: (i, 0)),
        out_shape=jax.ShapeDtypeStruct((rows, width), jnp.bfloat16),
        compiler_params=VMEM,
        name="modulate",
    )(tokens, shift_mod.reshape(1, width), scale_mod.reshape(1, width))


def project_kernel(norm_ref, w_ref, mask_ref, gain_ref, q_ref, kv_ref, sq_ref, acc_ref):
    which, half = pl.program_id(0), pl.program_id(1)
    depth = w_ref.shape[0] * w_ref.shape[2]
    cols = w_ref.shape[3]
    weight = w_ref[...].reshape(depth, cols)
    pieces = []
    blocks = depth // BLK
    for r in range(blocks):
        row = []
        for c in range(cols // BLK):
            kept = mask_ref[which, half * blocks + r, c]
            piece = weight[r * BLK : (r + 1) * BLK, c * BLK : (c + 1) * BLK]
            row.append(piece * kept.astype(jnp.float32).astype(jnp.bfloat16))
        pieces.append(jnp.concatenate(row, axis=1))
    pruned = jnp.concatenate(pieces, axis=0)
    part = jnp.dot(norm_ref[...], pruned, preferred_element_type=jnp.float32)

    @pl.when(half == 0)
    def _():
        acc_ref[...] = part

    @pl.when(half == 1)
    def _():
        total = acc_ref[...] + part
        scaled = total * gain_ref[0]
        sq_ref[0] = lax.dot_general(
            jnp.ones((8, cols), jnp.float32),
            total * total,
            (((1,), (1,)), ((), ())),
            precision=lax.Precision.HIGHEST,
            preferred_element_type=jnp.float32,
        )

        @pl.when(which == 0)
        def _():
            q_ref[...] = scaled

        @pl.when(which > 0)
        def _():
            kv_ref[...] = scaled.astype(jnp.bfloat16)


def project(normed, weights, masks, gains):
    rows, width = normed.shape
    parts, halves, depth, cols3 = weights.shape
    cols = cols3 // 3
    return pl.pallas_call(
        project_kernel,
        grid=(3, 2),
        in_specs=[
            pl.BlockSpec((rows, width // 2), lambda m, x: (0, x)),
            pl.BlockSpec((parts, 1, depth, cols), lambda m, x: (0, x, 0, m)),
            pl.BlockSpec(memory_space=pltpu.SMEM),
            pl.BlockSpec((1, 1, cols), lambda m, x: (m, 0, 0)),
        ],
        out_specs=[
            pl.BlockSpec((rows, cols), lambda m, x: (0, 0)),
            pl.BlockSpec((rows, cols), lambda m, x: (0, jnp.maximum(m - 1, 0))),
            pl.BlockSpec((1, 8, rows), lambda m, x: (m, 0, 0)),
        ],
        out_shape=[
            jax.ShapeDtypeStruct((rows, cols), jnp.float32),
            jax.ShapeDtypeStruct((rows, 2 * cols), jnp.bfloat16),
            jax.ShapeDtypeStruct((3, 8, rows), jnp.float32),
        ],
        scratch_shapes=[pltpu.VMEM((rows, cols), jnp.float32)],
        compiler_params=VMEM,
        name="project",
    )(normed, weights, masks, gains)


def attend_kernel(frame_ref, q_ref, rq_ref, kv0_ref, kv1_ref, kv2_ref, rk_ref, out_ref):
    cols = q_ref.shape[1]
    frame = frame_ref[0]
    kvs = (kv0_ref, kv1_ref, kv2_ref)
    for h in range(cols // HD):
        span = slice(h * HD, (h + 1) * HD)
        vspan = slice(cols + h * HD, cols + (h + 1) * HD)
        query = (q_ref[:, span] * rq_ref[...]).astype(jnp.bfloat16)
        scores = []
        for back, kv in enumerate(kvs):
            dots = lax.dot_general(
                query, kv[:, span], (((1,), (1,)), ((), ())), preferred_element_type=jnp.float32
            )
            scaled = dots * rk_ref[back : back + 1, :]
            if back < 2:
                scaled = jnp.where(frame >= 2 - back, scaled, neg_large)
            scores.append(scaled)
        top = jnp.maximum(
            jnp.maximum(
                jnp.max(scores[0], axis=1, keepdims=True), jnp.max(scores[1], axis=1, keepdims=True)
            ),
            jnp.max(scores[2], axis=1, keepdims=True),
        )
        total = 0.0
        mixed = 0.0
        for s, kv in zip(scores, kvs):
            grown = jnp.exp2(s - top)
            total = total + jnp.sum(grown, axis=1, keepdims=True)
            mixed = mixed + jnp.dot(
                grown.astype(jnp.bfloat16), kv[:, vspan], preferred_element_type=jnp.float32
            )
        out_ref[:, span] = (mixed / total).astype(jnp.bfloat16)


def attend(frame, q, rq, kv0, kv1, kv2, rk):
    rows, cols = q.shape
    whole = pl.BlockSpec(memory_space=pltpu.VMEM)
    return pl.pallas_call(
        attend_kernel,
        in_specs=[pl.BlockSpec(memory_space=pltpu.SMEM)] + [whole] * 6,
        out_specs=whole,
        out_shape=jax.ShapeDtypeStruct((rows, cols), jnp.bfloat16),
        compiler_params=VMEM,
        name="attend",
    )(frame, q, rq, kv0, kv1, kv2, rk)


def passed_along(block, distance):
    devices = range(lax.axis_size("tm"))
    route = [(i - distance, i) for i in devices if i - distance in devices]
    return lax.ppermute(block, "tm", route)


def shards_on(mesh):
    xs, zs, cs = grid_of(mesh)

    def tm(x, z, c):
        return (x * zs + z % zs) * cs + c

    x_swap = [(tm(x, z, c), tm(1 - x, z, c)) for x in range(xs) for z in range(zs) for c in range(cs)]
    zc_groups = [[tm(x, z, c) for z in range(zs) for c in range(cs)] for x in range(xs)]

    def shards(
        tokens, shift_mod, scale_mod, w_query, w_key, w_value, prune_masks, query_gain, key_gain
    ):
        frame = lax.axis_index("tm")
        x_at = frame // (zs * cs)
        mine = jnp.concatenate([w_query, w_key, w_value], axis=1)
        other = lax.ppermute(mine, "tm", x_swap)
        first = x_at == 0
        both = jnp.concatenate(
            [jnp.where(first, mine, other), jnp.where(first, other, mine)], axis=0
        )
        weights = lax.all_gather(both, "tm", axis=0, tiled=True, axis_index_groups=zc_groups)
        weights = weights.reshape(zs * cs, xs, mine.shape[0], mine.shape[1])
        normed = modulate(tokens, shift_mod, scale_mod)
        gains = jnp.stack([query_gain, key_gain, jnp.ones_like(key_gain)])[:, None, :]
        q, kv, sums = project(normed, weights, prune_masks, gains)
        one_back = passed_along(kv, 1)
        two_back = passed_along(kv, 2)
        totals = lax.psum(sums[:2, 0, :], "tensor")
        scales = lax.rsqrt(totals / float(HEADS * HD) + eps_rms)
        rk = scales[1] * (HD**-0.5 * LOG2E)
        rk1 = passed_along(rk, 1)
        rk2 = passed_along(rk, 2)
        rks = jnp.stack([rk2, rk1, rk])
        return attend(frame.reshape(1), q, scales[0][:, None], two_back, one_back, kv, rks)

    return shards


def solution(mesh):
    return jax.shard_map(
        shards_on(mesh),
        mesh=mesh,
        in_specs=(
            P("tm", None),
            P(),
            P(),
            P("tm", "tensor"),
            P("tm", "tensor"),
            P("tm", "tensor"),
            P(None, None, "tensor"),
            P("tensor"),
            P("tensor"),
        ),
        out_specs=P("tm", "tensor"),
        check_vma=False,
    )
```

```python
import jax
import jax.numpy as jnp
from jax import lax
from jax.experimental import pallas as pl
from jax.experimental.pallas import tpu as pltpu
from jax.sharding import PartitionSpec as P

HEADS = 24
HD = 128
BLK = 128
LOG2E = 1.4426950408889634

eps_layer = 1e-06
eps_rms = 1e-06
neg_large = -1e30
VMEM = pltpu.CompilerParams(vmem_limit_bytes=56 * 1024 * 1024)


def grid_of(mesh):
    return 2, mesh.shape["tm"] // 4, 2


def norm_kernel(tok_ref, shift_ref, scale_ref, out_ref):
    values = tok_ref[...].astype(jnp.float32)
    width = values.shape[1]
    average = jnp.sum(values, axis=1, keepdims=True) * (1.0 / width)
    centred = values - average
    variance = jnp.sum(centred * centred, axis=1, keepdims=True) * (1.0 / width)
    normalized = centred * lax.rsqrt(variance + eps_layer)
    out_ref[...] = (normalized * (1.0 + scale_ref[...]) + shift_ref[...]).astype(jnp.bfloat16)


def modulate(tokens, shift_mod, scale_mod):
    rows, width = tokens.shape
    step = 64
    return pl.pallas_call(
        norm_kernel,
        grid=(rows // step,),
        in_specs=[
            pl.BlockSpec((step, width), lambda i: (i, 0)),
            pl.BlockSpec((1, width), lambda i: (0, 0)),
            pl.BlockSpec((1, width), lambda i: (0, 0)),
        ],
        out_specs=pl.BlockSpec((step, width), lambda i: (i, 0)),
        out_shape=jax.ShapeDtypeStruct((rows, width), jnp.bfloat16),
        compiler_params=VMEM,
        name="modulate",
    )(tokens, shift_mod.reshape(1, width), scale_mod.reshape(1, width))


def masked(weight, mask_ref, which, first_block):
    rows, cols = weight.shape
    pieces = []
    for r in range(rows // BLK):
        row = []
        for c in range(cols // BLK):
            matrix, col = which(c)
            kept = mask_ref[matrix, first_block + r, col].astype(jnp.float32).astype(jnp.bfloat16)
            row.append(weight[r * BLK : (r + 1) * BLK, c * BLK : (c + 1) * BLK] * kept)
        pieces.append(jnp.concatenate(row, axis=1))
    return jnp.concatenate(pieces, axis=0)


def project_qk_kernel(norm_ref, w_ref, mask_ref, gain_ref, q_ref, k_ref, sq_ref, acc_ref):
    step = pl.program_id(0)
    depth = w_ref.shape[0] * w_ref.shape[2]
    cols = q_ref.shape[1]
    heads = cols // BLK
    blocks = depth // BLK
    weight = w_ref[...].reshape(depth, 2 * cols)
    pruned = masked(weight, mask_ref, lambda c: (c // heads, c % heads), step * blocks)
    part = jnp.dot(norm_ref[...], pruned, preferred_element_type=jnp.float32)

    @pl.when(step == 0)
    def _():
        acc_ref[...] = part

    @pl.when(step > 0)
    def _():
        acc_ref[...] += part

    @pl.when(step == pl.num_programs(0) - 1)
    def _():
        for m in range(2):
            total = acc_ref[:, m * cols : (m + 1) * cols]
            sums = lax.dot_general(
                jnp.ones((8, cols), jnp.float32),
                total * total,
                (((1,), (1,)), ((), ())),
                precision=lax.Precision.HIGHEST,
                preferred_element_type=jnp.float32,
            )
            sq_ref[m : m + 1, :] = sums[:1]
            scaled = total * gain_ref[m : m + 1, :]
            if m == 0:
                q_ref[...] = scaled
            else:
                k_ref[...] = scaled.astype(jnp.bfloat16)


def project_qk(normed, weights, masks, gains):
    rows, width = normed.shape
    parts, halves, depth, cols2 = weights.shape
    cols = cols2 // 2
    group = 8
    steps = parts // group
    return pl.pallas_call(
        project_qk_kernel,
        grid=(halves * steps,),
        in_specs=[
            pl.BlockSpec((rows, group * depth), lambda i: (0, i)),
            pl.BlockSpec((group, 1, depth, cols2), lambda i: (i % steps, i // steps, 0, 0)),
            pl.BlockSpec(memory_space=pltpu.SMEM),
            pl.BlockSpec((2, cols), lambda i: (0, 0)),
        ],
        out_specs=[
            pl.BlockSpec((rows, cols), lambda i: (0, 0)),
            pl.BlockSpec((rows, cols), lambda i: (0, 0)),
            pl.BlockSpec((2, rows), lambda i: (0, 0)),
        ],
        out_shape=[
            jax.ShapeDtypeStruct((rows, cols), jnp.float32),
            jax.ShapeDtypeStruct((rows, cols), jnp.bfloat16),
            jax.ShapeDtypeStruct((2, rows), jnp.float32),
        ],
        scratch_shapes=[pltpu.VMEM((rows, cols2), jnp.float32)],
        compiler_params=VMEM,
        name="project_qk",
    )(normed, weights, masks, gains)


def project_v_kernel(at_ref, norm_ref, w00_ref, w01_ref, w10_ref, w11_ref, mask_ref, v_ref, w_ref):
    cols = v_ref.shape[1]
    depth = 80
    chips = w00_ref.shape[0] // depth
    for i, j, piece_ref in ((0, 0, w00_ref), (0, 1, w01_ref), (1, 0, w10_ref), (1, 1, w11_ref)):
        x_at = jnp.abs(at_ref[0] - i)
        core = jnp.abs(at_ref[1] - j)
        for z in range(chips):
            row = pl.multiple_of(((x_at * chips + z) * 2 + core) * depth, 16)
            w_ref[pl.ds(row, depth), :] = piece_ref[z * depth : (z + 1) * depth, :]
    pruned = masked(w_ref[...], mask_ref, lambda c: (2, c), 0)
    v_ref[...] = jnp.dot(norm_ref[...], pruned, preferred_element_type=jnp.float32).astype(
        jnp.bfloat16
    )


def project_v(at, normed, pieces, masks):
    rows, width = normed.shape
    cols = pieces[0].shape[1]
    whole = pl.BlockSpec(memory_space=pltpu.VMEM)
    smem = pl.BlockSpec(memory_space=pltpu.SMEM)
    return pl.pallas_call(
        project_v_kernel,
        in_specs=[smem, whole, whole, whole, whole, whole, smem],
        out_specs=whole,
        out_shape=jax.ShapeDtypeStruct((rows, cols), jnp.bfloat16),
        scratch_shapes=[pltpu.VMEM((width, cols), jnp.bfloat16)],
        compiler_params=VMEM,
        name="project_v",
    )(at, normed, *pieces, masks)


def attend_kernel(
    frame_ref, q_ref, k0_ref, k1_ref, k2_ref, v0_ref, v1_ref, v2_ref, t0_ref, t1_ref, t2_ref, out_ref
):
    rows, cols = q_ref.shape
    frame = frame_ref[0]
    ks, vs, ts = (k0_ref, k1_ref, k2_ref), (v0_ref, v1_ref, v2_ref), (t0_ref, t1_ref, t2_ref)

    def scale_of(sums):
        return lax.rsqrt(sums * (1.0 / float(HEADS * HD)) + eps_rms)

    rq = jnp.transpose(jnp.broadcast_to(scale_of(t2_ref[0:1, :]), (8, rows)))[:, :1]
    rks = [scale_of(t[1:2, :]) * (HD**-0.5 * LOG2E) for t in ts]
    for h in range(cols // HD):
        span = slice(h * HD, (h + 1) * HD)
        query = (q_ref[:, span] * rq).astype(jnp.bfloat16)
        scores = []
        for back, key in enumerate(ks):
            dots = lax.dot_general(
                query, key[:, span], (((1,), (1,)), ((), ())), preferred_element_type=jnp.float32
            )
            scaled = dots * rks[back]
            if back < 2:
                scaled = jnp.where(frame >= 2 - back, scaled, neg_large)
            scores.append(scaled)
        top = jnp.maximum(
            jnp.maximum(
                jnp.max(scores[0], axis=1, keepdims=True), jnp.max(scores[1], axis=1, keepdims=True)
            ),
            jnp.max(scores[2], axis=1, keepdims=True),
        )
        total = 0.0
        mixed = 0.0
        for s, value in zip(scores, vs):
            grown = jnp.exp2(s - top)
            total = total + jnp.sum(grown, axis=1, keepdims=True)
            mixed = mixed + jnp.dot(
                grown.astype(jnp.bfloat16), value[:, span], preferred_element_type=jnp.float32
            )
        out_ref[:, span] = (mixed / total).astype(jnp.bfloat16)


def attend(frame, q, ks, vs, ts):
    rows, cols = q.shape
    whole = pl.BlockSpec(memory_space=pltpu.VMEM)
    return pl.pallas_call(
        attend_kernel,
        in_specs=[pl.BlockSpec(memory_space=pltpu.SMEM)] + [whole] * 10,
        out_specs=whole,
        out_shape=jax.ShapeDtypeStruct((rows, cols), jnp.bfloat16),
        compiler_params=VMEM,
        name="attend",
    )(frame, q, *ks, *vs, *ts)


def passed_along(block, distance):
    devices = range(lax.axis_size("tm"))
    route = [(i - distance, i) for i in devices if i - distance in devices]
    return lax.ppermute(block, "tm", route)


def shards_on(mesh):
    xs, zs, cs = grid_of(mesh)
    everyone = [(x, z, c) for x in range(xs) for z in range(zs) for c in range(cs)]

    def tm(x, z, c):
        return (x * zs + z % zs) * cs + c

    x_swap = [(tm(x, z, c), tm(1 - x, z, c)) for x, z, c in everyone]
    core_swap = [(tm(x, z, c), tm(x, z, 1 - c)) for x, z, c in everyone]
    zc_groups = [[tm(x, z, c) for z in range(zs) for c in range(cs)] for x in range(xs)]
    z_groups = [[tm(x, z, c) for z in range(zs)] for x in range(xs) for c in range(cs)]

    def swapped(block, route):
        return lax.ppermute(block, "tm", route)

    def shards(
        tokens, shift_mod, scale_mod, w_query, w_key, w_value, prune_masks, query_gain, key_gain
    ):
        frame = lax.axis_index("tm")
        x_at = frame // (zs * cs)
        mine = jnp.concatenate([w_query, w_key], axis=1)
        other = swapped(mine, x_swap)
        first = x_at == 0
        both = jnp.concatenate(
            [jnp.where(first, mine, other), jnp.where(first, other, mine)], axis=0
        )
        weights = lax.all_gather(both, "tm", axis=0, tiled=True, axis_index_groups=zc_groups)
        weights = weights.reshape(zs * cs, xs, mine.shape[0], mine.shape[1])
        normed = modulate(tokens, shift_mod, scale_mod)

        own_v = lax.all_gather(w_value, "tm", axis=0, tiled=True, axis_index_groups=z_groups)
        across_v = swapped(own_v, x_swap)
        beside_v = swapped(own_v, core_swap)
        both_v = swapped(across_v, core_swap)
        at = jnp.stack([x_at, frame % cs])
        values = project_v(at, normed, (own_v, beside_v, across_v, both_v), prune_masks)
        one_value, two_value = passed_along(values, 1), passed_along(values, 2)

        gains = jnp.stack([query_gain, key_gain])
        q, keys, sums = project_qk(normed, weights, prune_masks, gains)
        one_key, two_key = passed_along(keys, 1), passed_along(keys, 2)
        totals = lax.psum(sums, "tensor")
        one_total, two_total = passed_along(totals, 1), passed_along(totals, 2)
        return attend(
            frame.reshape(1),
            q,
            (two_key, one_key, keys),
            (two_value, one_value, values),
            (two_total, one_total, totals),
        )

    return shards


def solution(mesh):
    return jax.shard_map(
        shards_on(mesh),
        mesh=mesh,
        in_specs=(
            P("tm", None),
            P(),
            P(),
            P("tm", "tensor"),
            P("tm", "tensor"),
            P("tm", "tensor"),
            P(None, None, "tensor"),
            P("tensor"),
            P("tensor"),
        ),
        out_specs=P("tm", "tensor"),
        check_vma=False,
    )
```

```python
import jax
import jax.numpy as jnp
from jax import lax
from jax.experimental import pallas as pl
from jax.experimental.pallas import tpu as pltpu
from jax.sharding import PartitionSpec as P

HEADS = 24
HD = 128
BLK = 128
DEPTH = 80
CHUNK = 16
LOG2E = 1.4426950408889634

eps_layer = 1e-06
eps_rms = 1e-06
neg_large = -1e30
MIB = 1024 * 1024


def grid_of(mesh):
    return 2, mesh.shape["tm"] // 4, 2


def norm_kernel(tok_ref, shift_ref, scale_ref, out_ref):
    values = tok_ref[...].astype(jnp.float32)
    width = values.shape[1]
    average = jnp.sum(values, axis=1, keepdims=True) * (1.0 / width)
    centred = values - average
    variance = jnp.sum(centred * centred, axis=1, keepdims=True) * (1.0 / width)
    normalized = centred * lax.rsqrt(variance + eps_layer)
    out_ref[...] = (normalized * (1.0 + scale_ref[...]) + shift_ref[...]).astype(jnp.bfloat16)


def modulate(tokens, shift_mod, scale_mod):
    rows, width = tokens.shape
    step = 64
    return pl.pallas_call(
        norm_kernel,
        grid=(rows // step,),
        in_specs=[
            pl.BlockSpec((step, width), lambda i: (i, 0)),
            pl.BlockSpec((1, width), lambda i: (0, 0)),
            pl.BlockSpec((1, width), lambda i: (0, 0)),
        ],
        out_specs=pl.BlockSpec((step, width), lambda i: (i, 0)),
        out_shape=jax.ShapeDtypeStruct((rows, width), jnp.bfloat16),
        compiler_params=pltpu.CompilerParams(vmem_limit_bytes=16 * MIB),
        name="modulate",
    )(tokens, shift_mod.reshape(1, width), scale_mod.reshape(1, width))


def masked(weight, mask_ref, matrix, first_block):
    rows, cols = weight.shape
    pieces = []
    for r in range(rows // BLK):
        row = []
        for c in range(cols // BLK):
            kept = mask_ref[matrix, first_block + r, c] > 0
            block = weight[r * BLK : (r + 1) * BLK, c * BLK : (c + 1) * BLK]
            row.append(jnp.where(kept, block, jnp.zeros_like(block)))
        pieces.append(jnp.concatenate(row, axis=1))
    return jnp.concatenate(pieces, axis=0)


def row_sums(total):
    rows = total.shape[0]
    sums = jnp.sum(total * total, axis=1, keepdims=True)
    return jnp.transpose(jnp.broadcast_to(sums, (rows, 128)))[:1]


def gathered_product(matrix_at, matrix, norm_ref, w_hbm, mask_ref, w_buf, w_sem):
    parts, halves, _, depth, cols = w_hbm.shape
    steps, chunk = w_buf.shape[:2]
    rows = chunk * depth
    copies = []
    for i in range(steps):
        x, j = i // (steps // halves), i % (steps // halves)
        source = w_hbm.at[pl.ds(j * chunk, chunk), x, matrix_at]
        copies.append(pltpu.make_async_copy(source, w_buf.at[i], w_sem.at[i]))
    ahead = 2
    for copy in copies[:ahead]:
        copy.start()
    total = None
    for i, copy in enumerate(copies):
        copy.wait()
        if i + ahead < steps:
            copies[i + ahead].start()
        pruned = masked(w_buf[i].reshape(rows, cols), mask_ref, matrix, i * (rows // BLK))
        part = jnp.dot(
            norm_ref[:, i * rows : (i + 1) * rows], pruned, preferred_element_type=jnp.float32
        )
        total = part if total is None else total + part
    return total


def project_q_kernel(
    norm_ref, w_hbm, mask_ref, gain_ref, k0_ref, k1_ref, k2_ref, q_ref, sq_ref, w_buf, w_sem
):
    total = gathered_product(0, 0, norm_ref, w_hbm, mask_ref, w_buf, w_sem)
    q_ref[...] = total * gain_ref[...]
    sq_ref[0:1, :] = k0_ref[...]
    sq_ref[1:2, :] = k1_ref[...]
    sq_ref[2:3, :] = k2_ref[...]
    sq_ref[3:4, :] = row_sums(total)


def project_v_kernel(norm_ref, w_hbm, mask_ref, v_ref, w_buf, w_sem):
    total = gathered_product(1, 2, norm_ref, w_hbm, mask_ref, w_buf, w_sem)
    v_ref[...] = total.astype(jnp.bfloat16)


def project_gathered(normed, weights, masks, gain=None, key_sums=None):
    rows, width = normed.shape
    parts, halves, _, depth, cols = weights.shape
    chunk = CHUNK
    steps = halves * parts // chunk
    whole = pl.BlockSpec(memory_space=pltpu.VMEM)
    far = pl.BlockSpec(memory_space=pl.ANY)
    smem = pl.BlockSpec(memory_space=pltpu.SMEM)
    scratch = [
        pltpu.VMEM((steps, chunk, depth, cols), jnp.bfloat16),
        pltpu.SemaphoreType.DMA((steps,)),
    ]
    limit = pltpu.CompilerParams(vmem_limit_bytes=20 * MIB)
    if gain is None:
        return pl.pallas_call(
            project_v_kernel,
            in_specs=[whole, far, smem],
            out_specs=whole,
            out_shape=jax.ShapeDtypeStruct((rows, cols), jnp.bfloat16),
            scratch_shapes=scratch,
            compiler_params=limit,
            name="project_v",
        )(normed, weights, masks)
    return pl.pallas_call(
        project_q_kernel,
        in_specs=[whole, far, smem, whole, whole, whole, whole],
        out_specs=[whole, whole],
        out_shape=[
            jax.ShapeDtypeStruct((rows, cols), jnp.float32),
            jax.ShapeDtypeStruct((4, rows), jnp.float32),
        ],
        scratch_shapes=scratch,
        compiler_params=limit,
        name="project_q",
    )(normed, weights, masks, gain, *key_sums)


def project_k_kernel(
    at_ref, norm_ref, w00_ref, w01_ref, w10_ref, w11_ref, mask_ref, gain_ref, k_ref, sq_ref, w_buf
):
    halves, half, _ = w_buf.shape
    depth = DEPTH
    chips = w00_ref.shape[0] // depth
    for i, j, piece in ((0, 0, w00_ref), (0, 1, w01_ref), (1, 0, w10_ref), (1, 1, w11_ref)):
        core = jnp.abs(at_ref[1] - j)
        for z in range(chips):
            row = pl.multiple_of((z * 2 + core) * depth, 16)
            w_buf[i, pl.ds(row, depth), :] = piece[z * depth : (z + 1) * depth, :]
    total = None
    for i in range(halves):
        x_at = jnp.abs(at_ref[0] - i)
        pruned = masked(w_buf[i], mask_ref, 1, x_at * (half // BLK))
        columns = pl.ds(pl.multiple_of(x_at * half, BLK), half)
        part = jnp.dot(norm_ref[:, columns], pruned, preferred_element_type=jnp.float32)
        total = part if total is None else total + part
    k_ref[...] = (total * gain_ref[...]).astype(jnp.bfloat16)
    sq_ref[...] = row_sums(total)


def project_k(at, normed, pieces, masks, gain):
    rows, width = normed.shape
    cols = pieces[0].shape[1]
    whole = pl.BlockSpec(memory_space=pltpu.VMEM)
    smem = pl.BlockSpec(memory_space=pltpu.SMEM)
    return pl.pallas_call(
        project_k_kernel,
        in_specs=[smem, whole, whole, whole, whole, whole, smem, whole],
        out_specs=[whole, whole],
        out_shape=[
            jax.ShapeDtypeStruct((rows, cols), jnp.bfloat16),
            jax.ShapeDtypeStruct((1, rows), jnp.float32),
        ],
        scratch_shapes=[pltpu.VMEM((2, width // 2, cols), jnp.bfloat16)],
        compiler_params=pltpu.CompilerParams(vmem_limit_bytes=20 * MIB),
        name="project_k",
    )(at, normed, *pieces, masks, gain)


def attend_kernel(
    frame_ref, q_ref, k0_ref, k1_ref, k2_ref, v0_ref, v1_ref, v2_ref, totals_ref, out_ref
):
    rows, cols = q_ref.shape
    frame = frame_ref[0]
    ks, vs = (k0_ref, k1_ref, k2_ref), (v0_ref, v1_ref, v2_ref)
    scales = lax.rsqrt(totals_ref[...] * (1.0 / float(HEADS * HD)) + eps_rms)
    rq = jnp.transpose(jnp.broadcast_to(scales[3:4, :], (8, rows)))[:, :1]
    rks = scales * (HD**-0.5 * LOG2E)
    for h in range(cols // HD):
        span = slice(h * HD, (h + 1) * HD)
        query = (q_ref[:, span] * rq).astype(jnp.bfloat16)
        scores = []
        for back, key in enumerate(ks):
            dots = lax.dot_general(
                query, key[:, span], (((1,), (1,)), ((), ())), preferred_element_type=jnp.float32
            )
            scaled = dots * rks[back : back + 1, :]
            if back < 2:
                scaled = jnp.where(frame >= 2 - back, scaled, neg_large)
            scores.append(scaled)
        top = jnp.maximum(
            jnp.maximum(
                jnp.max(scores[0], axis=1, keepdims=True), jnp.max(scores[1], axis=1, keepdims=True)
            ),
            jnp.max(scores[2], axis=1, keepdims=True),
        )
        total = 0.0
        mixed = 0.0
        for s, value in zip(scores, vs):
            grown = jnp.exp2(s - top)
            total = total + jnp.sum(grown, axis=1, keepdims=True)
            mixed = mixed + jnp.dot(
                grown.astype(jnp.bfloat16), value[:, span], preferred_element_type=jnp.float32
            )
        out_ref[:, span] = (mixed / total).astype(jnp.bfloat16)


def attend(frame, q, ks, vs, totals):
    rows, cols = q.shape
    whole = pl.BlockSpec(memory_space=pltpu.VMEM)
    return pl.pallas_call(
        attend_kernel,
        in_specs=[pl.BlockSpec(memory_space=pltpu.SMEM)] + [whole] * 8,
        out_specs=whole,
        out_shape=jax.ShapeDtypeStruct((rows, cols), jnp.bfloat16),
        compiler_params=pltpu.CompilerParams(vmem_limit_bytes=28 * MIB),
        name="attend",
    )(frame, q, *ks, *vs, totals)


def passed_along(block, distance):
    devices = range(lax.axis_size("tm"))
    route = [(i - distance, i) for i in devices if i - distance in devices]
    return lax.ppermute(block, "tm", route)


def with_flipped(block, flip):
    size = lax.axis_size("tensor")
    return block + lax.ppermute(block, "tensor", [(i, i ^ flip) for i in range(size)])


def shards_on(mesh):
    xs, zs, cs = grid_of(mesh)
    everyone = [(x, z, c) for x in range(xs) for z in range(zs) for c in range(cs)]

    def tm(x, z, c):
        return (x * zs + z % zs) * cs + c

    x_swap = [(tm(x, z, c), tm(1 - x, z, c)) for x, z, c in everyone]
    core_swap = [(tm(x, z, c), tm(x, z, 1 - c)) for x, z, c in everyone]
    zc_groups = [[tm(x, z, c) for z in range(zs) for c in range(cs)] for x in range(xs)]
    z_groups = [[tm(x, z, c) for z in range(zs)] for x in range(xs) for c in range(cs)]

    def swapped(block, route):
        return lax.ppermute(block, "tm", route)

    def shards(
        tokens, shift_mod, scale_mod, w_query, w_key, w_value, prune_masks, query_gain, key_gain
    ):
        frame = lax.axis_index("tm")
        x_at = frame // (zs * cs)
        cols = w_query.shape[1]
        mine = jnp.concatenate([w_query, w_value], axis=0)
        other = swapped(mine, x_swap)
        first = x_at == 0
        both = jnp.concatenate(
            [jnp.where(first, mine, other), jnp.where(first, other, mine)], axis=0
        )
        weights = lax.all_gather(both, "tm", axis=0, tiled=True, axis_index_groups=zc_groups)
        weights = weights.reshape(zs * cs, xs, 2, w_query.shape[0], cols)

        own_k = lax.all_gather(w_key, "tm", axis=0, tiled=True, axis_index_groups=z_groups)
        across_k = swapped(own_k, x_swap)
        beside_k = swapped(own_k, core_swap)
        tokens, _ = lax.optimization_barrier((tokens, own_k))
        normed = modulate(tokens, shift_mod, scale_mod)
        across_k, normed = lax.optimization_barrier((across_k, normed))
        both_k = swapped(across_k, core_swap)
        at = jnp.stack([x_at, frame % cs])
        keys, key_sum = project_k(
            at, normed, (own_k, beside_k, across_k, both_k), prune_masks, key_gain[None, :]
        )
        one_sum, two_sum = passed_along(key_sum, 1), passed_along(key_sum, 2)
        one_key, two_key = passed_along(keys, 1), passed_along(keys, 2)

        q, sums = project_gathered(
            normed, weights, prune_masks, query_gain[None, :], (two_sum, one_sum, key_sum)
        )
        normed, _, one_key, two_key = lax.optimization_barrier((normed, q, one_key, two_key))
        totals = with_flipped(sums, 1)
        values = project_gathered(normed, weights, prune_masks)
        values, totals = lax.optimization_barrier((values, totals))
        one_value, two_value = passed_along(values, 1), passed_along(values, 2)
        flip = 2
        while flip < lax.axis_size("tensor"):
            totals = with_flipped(totals, flip)
            flip *= 2
        return attend(
            frame.reshape(1),
            q,
            (two_key, one_key, keys),
            (two_value, one_value, values),
            totals,
        )

    return shards


def solution(mesh):
    return jax.shard_map(
        shards_on(mesh),
        mesh=mesh,
        in_specs=(
            P("tm", None),
            P(),
            P(),
            P("tm", "tensor"),
            P("tm", "tensor"),
            P("tm", "tensor"),
            P(None, None, "tensor"),
            P("tensor"),
            P("tensor"),
        ),
        out_specs=P("tm", "tensor"),
        check_vma=False,
    )
```

```python
import jax
import jax.numpy as jnp
from jax import lax
from jax.experimental import pallas as pl
from jax.experimental.pallas import tpu as pltpu
from jax.sharding import PartitionSpec as P

HEADS = 24
HD = 128
BLK = 128
DEPTH = 80
LOG2E = 1.4426950408889634

eps_layer = 1e-06
eps_rms = 1e-06
neg_large = -1e30
MIB = 1024 * 1024


def grid_of(mesh):
    return 2, mesh.shape["tm"] // 4, 2


def norm_kernel(tok_ref, shift_ref, scale_ref, out_ref):
    values = tok_ref[...].astype(jnp.float32)
    width = values.shape[1]
    average = jnp.sum(values, axis=1, keepdims=True) * (1.0 / width)
    centred = values - average
    variance = jnp.sum(centred * centred, axis=1, keepdims=True) * (1.0 / width)
    normalized = centred * lax.rsqrt(variance + eps_layer)
    out_ref[...] = (normalized * (1.0 + scale_ref[...]) + shift_ref[...]).astype(jnp.bfloat16)


def modulate(tokens, shift_mod, scale_mod):
    rows, width = tokens.shape
    step = 64
    return pl.pallas_call(
        norm_kernel,
        grid=(rows // step,),
        in_specs=[
            pl.BlockSpec((step, width), lambda i: (i, 0)),
            pl.BlockSpec((1, width), lambda i: (0, 0)),
            pl.BlockSpec((1, width), lambda i: (0, 0)),
        ],
        out_specs=pl.BlockSpec((step, width), lambda i: (i, 0)),
        out_shape=jax.ShapeDtypeStruct((rows, width), jnp.bfloat16),
        compiler_params=pltpu.CompilerParams(vmem_limit_bytes=50 * MIB),
        name="modulate",
    )(tokens, shift_mod.reshape(1, width), scale_mod.reshape(1, width))


def masked(weight, mask_ref, matrices, first_block):
    rows, cols = weight.shape
    blocks = cols // BLK // len(matrices)
    pieces = []
    for r in range(rows // BLK):
        row = []
        for c in range(cols // BLK):
            kept = mask_ref[matrices[c // blocks], first_block + r, c % blocks] > 0
            block = weight[r * BLK : (r + 1) * BLK, c * BLK : (c + 1) * BLK]
            row.append(jnp.where(kept, block, jnp.zeros_like(block)))
        pieces.append(jnp.concatenate(row, axis=1))
    return jnp.concatenate(pieces, axis=0)


def row_sums(total):
    rows = total.shape[0]
    sums = jnp.sum(total * total, axis=1, keepdims=True)
    return jnp.transpose(jnp.broadcast_to(sums, (rows, 128)))[:1]


def project_qv_kernel(
    norm_ref, w_ref, mask_ref, gain_ref, k0_ref, k1_ref, sum_ref, q_ref, v_ref, sq_ref, acc_ref
):
    half = pl.program_id(0)
    parts, _, depth, cols = w_ref.shape
    rows = parts * depth
    weight = w_ref[...].reshape(rows, cols)
    pruned = masked(weight, mask_ref, (0, 2), half * (rows // BLK))
    part = jnp.dot(norm_ref[...], pruned, preferred_element_type=jnp.float32)

    @pl.when(half == 0)
    def _():
        acc_ref[...] = part

    @pl.when(half > 0)
    def _():
        total = acc_ref[...] + part
        query = total[:, : cols // 2]
        q_ref[...] = query * gain_ref[0:1, :]
        v_ref[...] = total[:, cols // 2 :].astype(jnp.bfloat16)
        ungain = 1.0 / gain_ref[1:2, :]
        sq_ref[0:1, :] = row_sums(k0_ref[...].astype(jnp.float32) * ungain)
        sq_ref[1:2, :] = row_sums(k1_ref[...].astype(jnp.float32) * ungain)
        sq_ref[2:3, :] = sum_ref[...]
        sq_ref[3:4, :] = row_sums(query)


def project_qv(normed, weights, masks, gains, two_key, one_key, key_sum):
    rows, width = normed.shape
    parts, halves, depth, cols2 = weights.shape
    cols = cols2 // 2

    def fixed(*shape):
        return pl.BlockSpec(shape, lambda i: (0, 0))

    return pl.pallas_call(
        project_qv_kernel,
        grid=(halves,),
        in_specs=[
            pl.BlockSpec((rows, width // halves), lambda i: (0, i)),
            pl.BlockSpec((parts, 1, depth, cols2), lambda i: (0, i, 0, 0)),
            pl.BlockSpec(memory_space=pltpu.SMEM),
            fixed(2, cols),
            fixed(rows, cols),
            fixed(rows, cols),
            fixed(1, rows),
        ],
        out_specs=[fixed(rows, cols), fixed(rows, cols), fixed(4, rows)],
        out_shape=[
            jax.ShapeDtypeStruct((rows, cols), jnp.float32),
            jax.ShapeDtypeStruct((rows, cols), jnp.bfloat16),
            jax.ShapeDtypeStruct((4, rows), jnp.float32),
        ],
        scratch_shapes=[pltpu.VMEM((rows, cols2), jnp.float32)],
        compiler_params=pltpu.CompilerParams(vmem_limit_bytes=52 * MIB),
        name="project_qv",
    )(normed, weights, masks, gains, two_key, one_key, key_sum)


def project_k_kernel(
    at_ref, norm_hbm, w00_ref, w01_ref, w10_ref, w11_ref, mask_ref, gain_ref, k_ref, sq_ref,
    norm_buf, w_buf, norm_sem,
):
    halves, half, _ = w_buf.shape
    depth = DEPTH
    chips = w00_ref.shape[0] // depth
    normed = pltpu.make_async_copy(norm_hbm, norm_buf, norm_sem)
    normed.start()
    for i, j, piece in ((0, 0, w00_ref), (0, 1, w01_ref), (1, 0, w10_ref), (1, 1, w11_ref)):
        core = jnp.abs(at_ref[1] - j)
        for z in range(chips):
            row = pl.multiple_of((z * 2 + core) * depth, 16)
            w_buf[i, pl.ds(row, depth), :] = piece[z * depth : (z + 1) * depth, :]
    normed.wait()
    total = None
    for i in range(halves):
        x_at = jnp.abs(at_ref[0] - i)
        pruned = masked(w_buf[i], mask_ref, (1,), x_at * (half // BLK))
        columns = pl.ds(pl.multiple_of(x_at * half, BLK), half)
        part = jnp.dot(norm_buf[:, columns], pruned, preferred_element_type=jnp.float32)
        total = part if total is None else total + part
    k_ref[...] = (total * gain_ref[...]).astype(jnp.bfloat16)
    sq_ref[...] = row_sums(total)


def project_k(at, normed, pieces, masks, gain):
    rows, width = normed.shape
    cols = pieces[0].shape[1]
    whole = pl.BlockSpec(memory_space=pltpu.VMEM)
    far = pl.BlockSpec(memory_space=pltpu.HBM)
    smem = pl.BlockSpec(memory_space=pltpu.SMEM)
    return pl.pallas_call(
        project_k_kernel,
        in_specs=[smem, far, whole, whole, whole, whole, smem, whole],
        out_specs=[whole, whole],
        out_shape=[
            jax.ShapeDtypeStruct((rows, cols), jnp.bfloat16),
            jax.ShapeDtypeStruct((1, rows), jnp.float32),
        ],
        scratch_shapes=[
            pltpu.VMEM((rows, width), jnp.bfloat16),
            pltpu.VMEM((2, width // 2, cols), jnp.bfloat16),
            pltpu.SemaphoreType.DMA,
        ],
        compiler_params=pltpu.CompilerParams(vmem_limit_bytes=50 * MIB),
        name="project_k",
    )(at, normed, *pieces, masks, gain)


def attend_kernel(
    frame_ref, q_ref, k0_ref, k1_ref, k2_ref, v0_ref, v1_ref, v2_ref, totals_ref, out_ref
):
    rows, cols = q_ref.shape
    frame = frame_ref[0]
    ks, vs = (k0_ref, k1_ref, k2_ref), (v0_ref, v1_ref, v2_ref)
    scales = lax.rsqrt(totals_ref[...] * (1.0 / float(HEADS * HD)) + eps_rms)
    rq = jnp.transpose(jnp.broadcast_to(scales[3:4, :], (8, rows)))[:, :1]
    rks = scales * (HD**-0.5 * LOG2E)
    for h in range(cols // HD):
        span = slice(h * HD, (h + 1) * HD)
        query = (q_ref[:, span] * rq).astype(jnp.bfloat16)
        scores = []
        for back, key in enumerate(ks):
            dots = lax.dot_general(
                query, key[:, span], (((1,), (1,)), ((), ())), preferred_element_type=jnp.float32
            )
            scaled = dots * rks[back : back + 1, :]
            if back < 2:
                scaled = jnp.where(frame >= 2 - back, scaled, neg_large)
            scores.append(scaled)
        top = jnp.maximum(
            jnp.maximum(
                jnp.max(scores[0], axis=1, keepdims=True), jnp.max(scores[1], axis=1, keepdims=True)
            ),
            jnp.max(scores[2], axis=1, keepdims=True),
        )
        total = 0.0
        mixed = 0.0
        for s, value in zip(scores, vs):
            grown = jnp.exp2(s - top)
            total = total + jnp.sum(grown, axis=1, keepdims=True)
            mixed = mixed + jnp.dot(
                grown.astype(jnp.bfloat16), value[:, span], preferred_element_type=jnp.float32
            )
        out_ref[:, span] = (mixed / total).astype(jnp.bfloat16)


def attend(frame, q, ks, vs, totals):
    rows, cols = q.shape
    whole = pl.BlockSpec(memory_space=pltpu.VMEM)
    return pl.pallas_call(
        attend_kernel,
        in_specs=[pl.BlockSpec(memory_space=pltpu.SMEM)] + [whole] * 8,
        out_specs=whole,
        out_shape=jax.ShapeDtypeStruct((rows, cols), jnp.bfloat16),
        compiler_params=pltpu.CompilerParams(vmem_limit_bytes=28 * MIB),
        name="attend",
    )(frame, q, *ks, *vs, totals)


def passed_along(block, distance):
    devices = range(lax.axis_size("tm"))
    route = [(i - distance, i) for i in devices if i - distance in devices]
    return lax.ppermute(block, "tm", route)


def with_others(block, group):
    size = lax.axis_size("tensor")
    flips = range(1, group) if group > 0 else range(-group, size, -group)
    shares = [lax.ppermute(block, "tensor", [(i, i ^ f) for i in range(size)]) for f in flips]
    return sum(shares, block)


def shards_on(mesh):
    xs, zs, cs = grid_of(mesh)
    everyone = [(x, z, c) for x in range(xs) for z in range(zs) for c in range(cs)]

    def tm(x, z, c):
        return (x * zs + z % zs) * cs + c

    x_swap = [(tm(x, z, c), tm(1 - x, z, c)) for x, z, c in everyone]
    core_swap = [(tm(x, z, c), tm(x, z, 1 - c)) for x, z, c in everyone]
    zc_groups = [[tm(x, z, c) for z in range(zs) for c in range(cs)] for x in range(xs)]
    z_groups = [[tm(x, z, c) for z in range(zs)] for x in range(xs) for c in range(cs)]

    def swapped(block, route):
        return lax.ppermute(block, "tm", route)

    def shards(
        tokens, shift_mod, scale_mod, w_query, w_key, w_value, prune_masks, query_gain, key_gain
    ):
        frame = lax.axis_index("tm")
        x_at = frame // (zs * cs)
        mine = jnp.concatenate([w_query, w_value], axis=1)
        other = swapped(mine, x_swap)
        first = x_at == 0
        both = jnp.concatenate(
            [jnp.where(first, mine, other), jnp.where(first, other, mine)], axis=0
        )
        weights = lax.all_gather(both, "tm", axis=0, tiled=True, axis_index_groups=zc_groups)
        weights = weights.reshape(zs * cs, xs, mine.shape[0], mine.shape[1])

        own_k = lax.all_gather(w_key, "tm", axis=0, tiled=True, axis_index_groups=z_groups)
        across_k = swapped(own_k, x_swap)
        beside_k = swapped(own_k, core_swap)
        normed = modulate(tokens, shift_mod, scale_mod)
        across_k, normed = lax.optimization_barrier((across_k, normed))
        both_k = swapped(across_k, core_swap)
        at = jnp.stack([x_at, frame % cs])
        keys, key_sum = project_k(
            at, normed, (own_k, beside_k, across_k, both_k), prune_masks, key_gain[None, :]
        )
        one_key, two_key = passed_along(keys, 1), passed_along(keys, 2)

        gains = jnp.stack([query_gain, key_gain])
        q, values, sums = project_qv(
            normed, weights, prune_masks, gains, two_key, one_key, key_sum
        )
        one_value, two_value = passed_along(values, 1), passed_along(values, 2)
        totals = with_others(with_others(sums, 2), -2)
        return attend(
            frame.reshape(1),
            q,
            (two_key, one_key, keys),
            (two_value, one_value, values),
            totals,
        )

    return shards


def solution(mesh):
    return jax.shard_map(
        shards_on(mesh),
        mesh=mesh,
        in_specs=(
            P("tm", None),
            P(),
            P(),
            P("tm", "tensor"),
            P("tm", "tensor"),
            P("tm", "tensor"),
            P(None, None, "tensor"),
            P("tensor"),
            P("tensor"),
        ),
        out_specs=P("tm", "tensor"),
        check_vma=False,
    )
```

```python
import jax
import jax.numpy as jnp
from jax import lax
from jax.experimental import pallas as pl
from jax.experimental.pallas import tpu as pltpu
from jax.sharding import PartitionSpec as P

HEADS = 24
HD = 128
BLK = 128
DEPTH = 80
LOG2E = 1.4426950408889634

eps_layer = 1e-06
eps_rms = 1e-06
neg_large = -1e30
MIB = 1024 * 1024


def grid_of(mesh):
    return 2, mesh.shape["tm"] // 4, 2


def norm_kernel(tok_ref, shift_ref, scale_ref, out_ref):
    values = tok_ref[...].astype(jnp.float32)
    width = values.shape[1]
    average = jnp.sum(values, axis=1, keepdims=True) * (1.0 / width)
    centred = values - average
    variance = jnp.sum(centred * centred, axis=1, keepdims=True) * (1.0 / width)
    normalized = centred * lax.rsqrt(variance + eps_layer)
    out_ref[...] = (normalized * (1.0 + scale_ref[...]) + shift_ref[...]).astype(jnp.bfloat16)


def modulate(tokens, shift_mod, scale_mod):
    rows, width = tokens.shape
    step = 64
    return pl.pallas_call(
        norm_kernel,
        grid=(rows // step,),
        in_specs=[
            pl.BlockSpec((step, width), lambda i: (i, 0)),
            pl.BlockSpec((1, width), lambda i: (0, 0)),
            pl.BlockSpec((1, width), lambda i: (0, 0)),
        ],
        out_specs=pl.BlockSpec((step, width), lambda i: (i, 0)),
        out_shape=jax.ShapeDtypeStruct((rows, width), jnp.bfloat16),
        compiler_params=pltpu.CompilerParams(vmem_limit_bytes=50 * MIB),
        name="modulate",
    )(tokens, shift_mod.reshape(1, width), scale_mod.reshape(1, width))


def masked(weight, mask_ref, matrices, first_block):
    rows, cols = weight.shape
    blocks = cols // BLK // len(matrices)
    pieces = []
    for r in range(rows // BLK):
        row = []
        for c in range(cols // BLK):
            kept = mask_ref[matrices[c // blocks], first_block + r, c % blocks] > 0
            block = weight[r * BLK : (r + 1) * BLK, c * BLK : (c + 1) * BLK]
            row.append(jnp.where(kept, block, jnp.zeros_like(block)))
        pieces.append(jnp.concatenate(row, axis=1))
    return jnp.concatenate(pieces, axis=0)


def row_sums(total):
    rows = total.shape[0]
    sums = jnp.sum(total * total, axis=1, keepdims=True)
    return jnp.transpose(jnp.broadcast_to(sums, (rows, 128)))[:1]


def project_qv_kernel(
    norm_ref, w_ref, mask_ref, gain_ref, k0_ref, k1_ref, k2_ref, q_ref, v_ref, sq_ref, acc_ref
):
    half = pl.program_id(0)
    parts, _, depth, cols = w_ref.shape
    rows = parts * depth
    weight = w_ref[...].reshape(rows, cols)
    pruned = masked(weight, mask_ref, (0, 2), half * (rows // BLK))
    part = jnp.dot(norm_ref[...], pruned, preferred_element_type=jnp.float32)

    @pl.when(half == 0)
    def _():
        acc_ref[...] = part

    @pl.when(half > 0)
    def _():
        total = acc_ref[...] + part
        query = total[:, : cols // 2]
        q_ref[...] = query * gain_ref[...]
        v_ref[...] = total[:, cols // 2 :].astype(jnp.bfloat16)
        sq_ref[0:1, :] = k0_ref[...]
        sq_ref[1:2, :] = k1_ref[...]
        sq_ref[2:3, :] = k2_ref[...]
        sq_ref[3:4, :] = row_sums(query)


def project_qv(normed, weights, masks, gain, key_sums):
    rows, width = normed.shape
    parts, halves, depth, cols2 = weights.shape
    cols = cols2 // 2

    def fixed(*shape):
        return pl.BlockSpec(shape, lambda i: (0, 0))

    return pl.pallas_call(
        project_qv_kernel,
        grid=(halves,),
        in_specs=[
            pl.BlockSpec((rows, width // halves), lambda i: (0, i)),
            pl.BlockSpec((parts, 1, depth, cols2), lambda i: (0, i, 0, 0)),
            pl.BlockSpec(memory_space=pltpu.SMEM),
            fixed(1, cols),
            fixed(1, rows),
            fixed(1, rows),
            fixed(1, rows),
        ],
        out_specs=[fixed(rows, cols), fixed(rows, cols), fixed(4, rows)],
        out_shape=[
            jax.ShapeDtypeStruct((rows, cols), jnp.float32),
            jax.ShapeDtypeStruct((rows, cols), jnp.bfloat16),
            jax.ShapeDtypeStruct((4, rows), jnp.float32),
        ],
        scratch_shapes=[pltpu.VMEM((rows, cols2), jnp.float32)],
        compiler_params=pltpu.CompilerParams(vmem_limit_bytes=52 * MIB),
        name="project_qv",
    )(normed, weights, masks, gain, *key_sums)


def project_k_kernel(
    at_ref, norm_hbm, w00_ref, w01_ref, w10_ref, w11_ref, mask_ref, gain_ref, k_ref, sq_ref,
    norm_buf, w_buf, norm_sem,
):
    halves, half, _ = w_buf.shape
    depth = DEPTH
    chips = w00_ref.shape[0] // depth
    normed = pltpu.make_async_copy(norm_hbm, norm_buf, norm_sem)
    normed.start()
    for i, j, piece in ((0, 0, w00_ref), (0, 1, w01_ref), (1, 0, w10_ref), (1, 1, w11_ref)):
        core = jnp.abs(at_ref[1] - j)
        for z in range(chips):
            row = pl.multiple_of((z * 2 + core) * depth, 16)
            w_buf[i, pl.ds(row, depth), :] = piece[z * depth : (z + 1) * depth, :]
    normed.wait()
    total = None
    for i in range(halves):
        x_at = jnp.abs(at_ref[0] - i)
        pruned = masked(w_buf[i], mask_ref, (1,), x_at * (half // BLK))
        columns = pl.ds(pl.multiple_of(x_at * half, BLK), half)
        part = jnp.dot(norm_buf[:, columns], pruned, preferred_element_type=jnp.float32)
        total = part if total is None else total + part
    k_ref[...] = (total * gain_ref[...]).astype(jnp.bfloat16)
    sq_ref[...] = row_sums(total)


def project_k(at, normed, pieces, masks, gain):
    rows, width = normed.shape
    cols = pieces[0].shape[1]
    whole = pl.BlockSpec(memory_space=pltpu.VMEM)
    far = pl.BlockSpec(memory_space=pltpu.HBM)
    smem = pl.BlockSpec(memory_space=pltpu.SMEM)
    return pl.pallas_call(
        project_k_kernel,
        in_specs=[smem, far, whole, whole, whole, whole, smem, whole],
        out_specs=[whole, whole],
        out_shape=[
            jax.ShapeDtypeStruct((rows, cols), jnp.bfloat16),
            jax.ShapeDtypeStruct((1, rows), jnp.float32),
        ],
        scratch_shapes=[
            pltpu.VMEM((rows, width), jnp.bfloat16),
            pltpu.VMEM((2, width // 2, cols), jnp.bfloat16),
            pltpu.SemaphoreType.DMA,
        ],
        compiler_params=pltpu.CompilerParams(vmem_limit_bytes=50 * MIB),
        name="project_k",
    )(at, normed, *pieces, masks, gain)


def attend_kernel(
    frame_ref, q_ref, k0_ref, k1_ref, k2_ref, v0_ref, v1_ref, v2_ref, totals_ref, out_ref
):
    rows, cols = q_ref.shape
    frame = frame_ref[0]
    ks, vs = (k0_ref, k1_ref, k2_ref), (v0_ref, v1_ref, v2_ref)
    scales = lax.rsqrt(totals_ref[...] * (1.0 / float(HEADS * HD)) + eps_rms)
    rq = jnp.transpose(jnp.broadcast_to(scales[3:4, :], (8, rows)))[:, :1]
    rks = scales * (HD**-0.5 * LOG2E)
    for h in range(cols // HD):
        span = slice(h * HD, (h + 1) * HD)
        query = (q_ref[:, span] * rq).astype(jnp.bfloat16)
        scores = []
        for back, key in enumerate(ks):
            dots = lax.dot_general(
                query, key[:, span], (((1,), (1,)), ((), ())), preferred_element_type=jnp.float32
            )
            scaled = dots * rks[back : back + 1, :]
            if back < 2:
                scaled = jnp.where(frame >= 2 - back, scaled, neg_large)
            scores.append(scaled)
        top = jnp.maximum(
            jnp.maximum(
                jnp.max(scores[0], axis=1, keepdims=True), jnp.max(scores[1], axis=1, keepdims=True)
            ),
            jnp.max(scores[2], axis=1, keepdims=True),
        )
        total = 0.0
        mixed = 0.0
        for s, value in zip(scores, vs):
            grown = jnp.exp2(s - top)
            total = total + jnp.sum(grown, axis=1, keepdims=True)
            mixed = mixed + jnp.dot(
                grown.astype(jnp.bfloat16), value[:, span], preferred_element_type=jnp.float32
            )
        out_ref[:, span] = (mixed / total).astype(jnp.bfloat16)


def attend(frame, q, ks, vs, totals):
    rows, cols = q.shape
    whole = pl.BlockSpec(memory_space=pltpu.VMEM)
    return pl.pallas_call(
        attend_kernel,
        in_specs=[pl.BlockSpec(memory_space=pltpu.SMEM)] + [whole] * 8,
        out_specs=whole,
        out_shape=jax.ShapeDtypeStruct((rows, cols), jnp.bfloat16),
        compiler_params=pltpu.CompilerParams(vmem_limit_bytes=28 * MIB),
        name="attend",
    )(frame, q, *ks, *vs, totals)


def passed_along(block, distance):
    devices = range(lax.axis_size("tm"))
    route = [(i - distance, i) for i in devices if i - distance in devices]
    return lax.ppermute(block, "tm", route)


def summed_over_tensor(block):
    size = lax.axis_size("tensor")
    routes = [[(i, i ^ flip) for i in range(size)] for flip in range(1, size)]
    return sum((lax.ppermute(block, "tensor", route) for route in routes), block)


def shards_on(mesh):
    xs, zs, cs = grid_of(mesh)
    everyone = [(x, z, c) for x in range(xs) for z in range(zs) for c in range(cs)]

    def tm(x, z, c):
        return (x * zs + z % zs) * cs + c

    x_swap = [(tm(x, z, c), tm(1 - x, z, c)) for x, z, c in everyone]
    core_swap = [(tm(x, z, c), tm(x, z, 1 - c)) for x, z, c in everyone]
    zc_groups = [[tm(x, z, c) for z in range(zs) for c in range(cs)] for x in range(xs)]
    z_groups = [[tm(x, z, c) for z in range(zs)] for x in range(xs) for c in range(cs)]

    def swapped(block, route):
        return lax.ppermute(block, "tm", route)

    def shards(
        tokens, shift_mod, scale_mod, w_query, w_key, w_value, prune_masks, query_gain, key_gain
    ):
        frame = lax.axis_index("tm")
        x_at = frame // (zs * cs)
        mine = jnp.concatenate([w_query, w_value], axis=1)
        other = swapped(mine, x_swap)
        first = x_at == 0
        both = jnp.concatenate(
            [jnp.where(first, mine, other), jnp.where(first, other, mine)], axis=0
        )
        weights = lax.all_gather(both, "tm", axis=0, tiled=True, axis_index_groups=zc_groups)
        weights = weights.reshape(zs * cs, xs, mine.shape[0], mine.shape[1])

        own_k = lax.all_gather(w_key, "tm", axis=0, tiled=True, axis_index_groups=z_groups)
        across_k = swapped(own_k, x_swap)
        beside_k = swapped(own_k, core_swap)
        normed = modulate(tokens, shift_mod, scale_mod)
        across_k, normed = lax.optimization_barrier((across_k, normed))
        both_k = swapped(across_k, core_swap)
        at = jnp.stack([x_at, frame % cs])
        keys, key_sum = project_k(
            at, normed, (own_k, beside_k, across_k, both_k), prune_masks, key_gain[None, :]
        )
        one_sum, two_sum = passed_along(key_sum, 1), passed_along(key_sum, 2)
        keys, one_sum, two_sum = lax.optimization_barrier((keys, one_sum, two_sum))
        one_key, two_key = passed_along(keys, 1), passed_along(keys, 2)

        q, values, sums = project_qv(
            normed, weights, prune_masks, query_gain[None, :], (two_sum, one_sum, key_sum)
        )
        sums, one_key, two_key = lax.optimization_barrier((sums, one_key, two_key))
        one_value, two_value = passed_along(values, 1), passed_along(values, 2)
        totals = summed_over_tensor(sums)
        return attend(
            frame.reshape(1),
            q,
            (two_key, one_key, keys),
            (two_value, one_value, values),
            totals,
        )

    return shards


def solution(mesh):
    return jax.shard_map(
        shards_on(mesh),
        mesh=mesh,
        in_specs=(
            P("tm", None),
            P(),
            P(),
            P("tm", "tensor"),
            P("tm", "tensor"),
            P("tm", "tensor"),
            P(None, None, "tensor"),
            P("tensor"),
            P("tensor"),
        ),
        out_specs=P("tm", "tensor"),
        check_vma=False,
    )
```

```python
import jax
import jax.numpy as jnp
from jax import lax
from jax.experimental import pallas as pl
from jax.experimental.pallas import tpu as pltpu
from jax.sharding import PartitionSpec as P

HEADS = 24
HD = 128
BLK = 128
DEPTH = 80
LOG2E = 1.4426950408889634

eps_layer = 1e-06
eps_rms = 1e-06
neg_large = -1e30
MIB = 1024 * 1024


def grid_of(mesh):
    return 2, mesh.shape["tm"] // 4, 2


def norm_kernel(tok_ref, shift_ref, scale_ref, out_ref):
    values = tok_ref[...].astype(jnp.float32)
    width = values.shape[1]
    average = jnp.sum(values, axis=1, keepdims=True) * (1.0 / width)
    centred = values - average
    variance = jnp.sum(centred * centred, axis=1, keepdims=True) * (1.0 / width)
    normalized = centred * lax.rsqrt(variance + eps_layer)
    out_ref[...] = (normalized * (1.0 + scale_ref[...]) + shift_ref[...]).astype(jnp.bfloat16)


def modulate(tokens, shift_mod, scale_mod):
    rows, width = tokens.shape
    step = 64
    return pl.pallas_call(
        norm_kernel,
        grid=(rows // step,),
        in_specs=[
            pl.BlockSpec((step, width), lambda i: (i, 0)),
            pl.BlockSpec((1, width), lambda i: (0, 0)),
            pl.BlockSpec((1, width), lambda i: (0, 0)),
        ],
        out_specs=pl.BlockSpec((step, width), lambda i: (i, 0)),
        out_shape=jax.ShapeDtypeStruct((rows, width), jnp.bfloat16),
        compiler_params=pltpu.CompilerParams(vmem_limit_bytes=50 * MIB),
        name="modulate",
    )(tokens, shift_mod.reshape(1, width), scale_mod.reshape(1, width))


def masked(weight, mask_ref, matrices, first_block):
    rows, cols = weight.shape
    blocks = cols // BLK // len(matrices)
    pieces = []
    for r in range(rows // BLK):
        row = []
        for c in range(cols // BLK):
            kept = mask_ref[matrices[c // blocks], first_block + r, c % blocks] > 0
            block = weight[r * BLK : (r + 1) * BLK, c * BLK : (c + 1) * BLK]
            row.append(jnp.where(kept, block, jnp.zeros_like(block)))
        pieces.append(jnp.concatenate(row, axis=1))
    return jnp.concatenate(pieces, axis=0)


def row_sums(total):
    rows = total.shape[0]
    sums = jnp.sum(total * total, axis=1, keepdims=True)
    return jnp.transpose(jnp.broadcast_to(sums, (rows, 128)))[:1]


def project_qv_kernel(
    norm_ref, w_ref, mask_ref, gain_ref, q_ref, v_ref, sq_ref, acc_ref
):
    half = pl.program_id(0)
    parts, _, depth, cols = w_ref.shape
    rows = parts * depth
    weight = w_ref[...].reshape(rows, cols)
    pruned = masked(weight, mask_ref, (0, 2), half * (rows // BLK))
    part = jnp.dot(norm_ref[...], pruned, preferred_element_type=jnp.float32)

    @pl.when(half == 0)
    def _():
        acc_ref[...] = part

    @pl.when(half > 0)
    def _():
        total = acc_ref[...] + part
        query = total[:, : cols // 2]
        q_ref[...] = query * gain_ref[...]
        v_ref[...] = total[:, cols // 2 :].astype(jnp.bfloat16)
        sq_ref[...] = row_sums(query)


def project_qv(normed, weights, masks, gain):
    rows, width = normed.shape
    parts, halves, depth, cols2 = weights.shape
    cols = cols2 // 2

    def fixed(*shape):
        return pl.BlockSpec(shape, lambda i: (0, 0))

    return pl.pallas_call(
        project_qv_kernel,
        grid=(halves,),
        in_specs=[
            pl.BlockSpec((rows, width // halves), lambda i: (0, i)),
            pl.BlockSpec((parts, 1, depth, cols2), lambda i: (0, i, 0, 0)),
            pl.BlockSpec(memory_space=pltpu.SMEM),
            fixed(1, cols),
        ],
        out_specs=[fixed(rows, cols), fixed(rows, cols), fixed(1, rows)],
        out_shape=[
            jax.ShapeDtypeStruct((rows, cols), jnp.float32),
            jax.ShapeDtypeStruct((rows, cols), jnp.bfloat16),
            jax.ShapeDtypeStruct((1, rows), jnp.float32),
        ],
        scratch_shapes=[pltpu.VMEM((rows, cols2), jnp.float32)],
        compiler_params=pltpu.CompilerParams(vmem_limit_bytes=52 * MIB),
        name="project_qv",
    )(normed, weights, masks, gain)


def project_k_kernel(
    at_ref, norm_hbm, w00_ref, w01_ref, w10_ref, w11_ref, mask_ref, gain_ref, k_ref, sq_ref,
    norm_buf, w_buf, norm_sem,
):
    halves, half, _ = w_buf.shape
    depth = DEPTH
    chips = w00_ref.shape[0] // depth
    normed = pltpu.make_async_copy(norm_hbm, norm_buf, norm_sem)
    normed.start()
    for i, j, piece in ((0, 0, w00_ref), (0, 1, w01_ref), (1, 0, w10_ref), (1, 1, w11_ref)):
        core = jnp.abs(at_ref[1] - j)
        for z in range(chips):
            row = pl.multiple_of((z * 2 + core) * depth, 16)
            w_buf[i, pl.ds(row, depth), :] = piece[z * depth : (z + 1) * depth, :]
    normed.wait()
    total = None
    for i in range(halves):
        x_at = jnp.abs(at_ref[0] - i)
        pruned = masked(w_buf[i], mask_ref, (1,), x_at * (half // BLK))
        columns = pl.ds(pl.multiple_of(x_at * half, BLK), half)
        part = jnp.dot(norm_buf[:, columns], pruned, preferred_element_type=jnp.float32)
        total = part if total is None else total + part
    k_ref[...] = (total * gain_ref[...]).astype(jnp.bfloat16)
    sq_ref[...] = row_sums(total)


def project_k(at, normed, pieces, masks, gain):
    rows, width = normed.shape
    cols = pieces[0].shape[1]
    whole = pl.BlockSpec(memory_space=pltpu.VMEM)
    far = pl.BlockSpec(memory_space=pltpu.HBM)
    smem = pl.BlockSpec(memory_space=pltpu.SMEM)
    return pl.pallas_call(
        project_k_kernel,
        in_specs=[smem, far, whole, whole, whole, whole, smem, whole],
        out_specs=[whole, whole],
        out_shape=[
            jax.ShapeDtypeStruct((rows, cols), jnp.bfloat16),
            jax.ShapeDtypeStruct((1, rows), jnp.float32),
        ],
        scratch_shapes=[
            pltpu.VMEM((rows, width), jnp.bfloat16),
            pltpu.VMEM((2, width // 2, cols), jnp.bfloat16),
            pltpu.SemaphoreType.DMA,
        ],
        compiler_params=pltpu.CompilerParams(vmem_limit_bytes=50 * MIB),
        name="project_k",
    )(at, normed, *pieces, masks, gain)


def attend_kernel(
    frame_ref, q_ref, k0_ref, k1_ref, k2_ref, v0_ref, v1_ref, v2_ref, totals_ref, out_ref
):
    rows, cols = q_ref.shape
    frame = frame_ref[0]
    ks, vs = (k0_ref, k1_ref, k2_ref), (v0_ref, v1_ref, v2_ref)
    scales = lax.rsqrt(totals_ref[...] * (1.0 / float(HEADS * HD)) + eps_rms)
    rq = jnp.transpose(jnp.broadcast_to(scales[3:4, :], (8, rows)))[:, :1]
    rks = scales * (HD**-0.5 * LOG2E)
    for h in range(cols // HD):
        span = slice(h * HD, (h + 1) * HD)
        query = (q_ref[:, span] * rq).astype(jnp.bfloat16)
        scores = []
        for back, key in enumerate(ks):
            dots = lax.dot_general(
                query, key[:, span], (((1,), (1,)), ((), ())), preferred_element_type=jnp.float32
            )
            scaled = dots * rks[back : back + 1, :]
            if back < 2:
                scaled = jnp.where(frame >= 2 - back, scaled, neg_large)
            scores.append(scaled)
        top = jnp.maximum(
            jnp.maximum(
                jnp.max(scores[0], axis=1, keepdims=True), jnp.max(scores[1], axis=1, keepdims=True)
            ),
            jnp.max(scores[2], axis=1, keepdims=True),
        )
        total = 0.0
        mixed = 0.0
        for s, value in zip(scores, vs):
            grown = jnp.exp2(s - top)
            total = total + jnp.sum(grown, axis=1, keepdims=True)
            mixed = mixed + jnp.dot(
                grown.astype(jnp.bfloat16), value[:, span], preferred_element_type=jnp.float32
            )
        out_ref[:, span] = (mixed / total).astype(jnp.bfloat16)


def attend(frame, q, ks, vs, totals):
    rows, cols = q.shape
    whole = pl.BlockSpec(memory_space=pltpu.VMEM)
    return pl.pallas_call(
        attend_kernel,
        in_specs=[pl.BlockSpec(memory_space=pltpu.SMEM)] + [whole] * 8,
        out_specs=whole,
        out_shape=jax.ShapeDtypeStruct((rows, cols), jnp.bfloat16),
        compiler_params=pltpu.CompilerParams(vmem_limit_bytes=28 * MIB),
        name="attend",
    )(frame, q, *ks, *vs, totals)


def passed_along(block, distance):
    devices = range(lax.axis_size("tm"))
    route = [(i - distance, i) for i in devices if i - distance in devices]
    return lax.ppermute(block, "tm", route)


def with_flipped(block, flip):
    size = lax.axis_size("tensor")
    return block + lax.ppermute(block, "tensor", [(i, i ^ flip) for i in range(size)])


def shards_on(mesh):
    xs, zs, cs = grid_of(mesh)
    everyone = [(x, z, c) for x in range(xs) for z in range(zs) for c in range(cs)]

    def tm(x, z, c):
        return (x * zs + z % zs) * cs + c

    x_swap = [(tm(x, z, c), tm(1 - x, z, c)) for x, z, c in everyone]
    core_swap = [(tm(x, z, c), tm(x, z, 1 - c)) for x, z, c in everyone]
    zc_groups = [[tm(x, z, c) for z in range(zs) for c in range(cs)] for x in range(xs)]
    z_groups = [[tm(x, z, c) for z in range(zs)] for x in range(xs) for c in range(cs)]

    def swapped(block, route):
        return lax.ppermute(block, "tm", route)

    def shards(
        tokens, shift_mod, scale_mod, w_query, w_key, w_value, prune_masks, query_gain, key_gain
    ):
        frame = lax.axis_index("tm")
        x_at = frame // (zs * cs)
        mine = jnp.concatenate([w_query, w_value], axis=1)
        other = swapped(mine, x_swap)
        first = x_at == 0
        both = jnp.concatenate(
            [jnp.where(first, mine, other), jnp.where(first, other, mine)], axis=0
        )
        weights = lax.all_gather(both, "tm", axis=0, tiled=True, axis_index_groups=zc_groups)
        weights = weights.reshape(zs * cs, xs, mine.shape[0], mine.shape[1])

        own_k = lax.all_gather(w_key, "tm", axis=0, tiled=True, axis_index_groups=z_groups)
        across_k = swapped(own_k, x_swap)
        beside_k = swapped(own_k, core_swap)
        normed = modulate(tokens, shift_mod, scale_mod)
        across_k, normed = lax.optimization_barrier((across_k, normed))
        both_k = swapped(across_k, core_swap)
        at = jnp.stack([x_at, frame % cs])
        keys, key_sum = project_k(
            at, normed, (own_k, beside_k, across_k, both_k), prune_masks, key_gain[None, :]
        )
        one_key, two_key = passed_along(keys, 1), passed_along(keys, 2)
        one_sum, two_sum = passed_along(key_sum, 1), passed_along(key_sum, 2)

        q, values, query_sum = project_qv(normed, weights, prune_masks, query_gain[None, :])
        query_sum, one_key, two_key, one_sum, two_sum = lax.optimization_barrier(
            (query_sum, one_key, two_key, one_sum, two_sum)
        )
        one_value = passed_along(values, 1)
        totals = with_flipped(jnp.concatenate([two_sum, one_sum, key_sum, query_sum]), 1)
        later_values, totals = lax.optimization_barrier((values, totals))
        two_value = passed_along(later_values, 2)
        flip = 2
        while flip < lax.axis_size("tensor"):
            totals = with_flipped(totals, flip)
            flip *= 2
        return attend(
            frame.reshape(1),
            q,
            (two_key, one_key, keys),
            (two_value, one_value, values),
            totals,
        )

    return shards


def solution(mesh):
    return jax.shard_map(
        shards_on(mesh),
        mesh=mesh,
        in_specs=(
            P("tm", None),
            P(),
            P(),
            P("tm", "tensor"),
            P("tm", "tensor"),
            P("tm", "tensor"),
            P(None, None, "tensor"),
            P("tensor"),
            P("tensor"),
        ),
        out_specs=P("tm", "tensor"),
        check_vma=False,
    )
```

```python
import jax
import jax.numpy as jnp
from jax import lax
from jax.experimental import pallas as pl
from jax.experimental.pallas import tpu as pltpu
from jax.sharding import PartitionSpec as P

HEADS = 24
HD = 128
BLK = 128
DEPTH = 80
LOG2E = 1.4426950408889634

eps_layer = 1e-06
eps_rms = 1e-06
neg_large = -1e30
MIB = 1024 * 1024


def grid_of(mesh):
    return 2, mesh.shape["tm"] // 4, 2


def norm_kernel(tok_ref, shift_ref, scale_ref, out_ref):
    values = tok_ref[...].astype(jnp.float32)
    width = values.shape[1]
    average = jnp.sum(values, axis=1, keepdims=True) * (1.0 / width)
    centred = values - average
    variance = jnp.sum(centred * centred, axis=1, keepdims=True) * (1.0 / width)
    normalized = centred * lax.rsqrt(variance + eps_layer)
    out_ref[...] = (normalized * (1.0 + scale_ref[...]) + shift_ref[...]).astype(jnp.bfloat16)


def modulate(tokens, shift_mod, scale_mod):
    rows, width = tokens.shape
    step = 64
    return pl.pallas_call(
        norm_kernel,
        grid=(rows // step,),
        in_specs=[
            pl.BlockSpec((step, width), lambda i: (i, 0)),
            pl.BlockSpec((1, width), lambda i: (0, 0)),
            pl.BlockSpec((1, width), lambda i: (0, 0)),
        ],
        out_specs=pl.BlockSpec((step, width), lambda i: (i, 0)),
        out_shape=jax.ShapeDtypeStruct((rows, width), jnp.bfloat16),
        compiler_params=pltpu.CompilerParams(vmem_limit_bytes=50 * MIB),
        name="modulate",
    )(tokens, shift_mod.reshape(1, width), scale_mod.reshape(1, width))


def masked(weights, mask_ref, matrices, first_block):
    pieces = []
    for r in range(weights[0].shape[0] // BLK):
        row = []
        for weight, matrix in zip(weights, matrices):
            for c in range(weight.shape[1] // BLK):
                kept = mask_ref[matrix, first_block + r, c] > 0
                block = weight[r * BLK : (r + 1) * BLK, c * BLK : (c + 1) * BLK]
                row.append(jnp.where(kept, block, jnp.zeros_like(block)))
        pieces.append(jnp.concatenate(row, axis=1))
    return jnp.concatenate(pieces, axis=0)


def row_sums(total):
    rows = total.shape[0]
    sums = jnp.sum(total * total, axis=1, keepdims=True)
    return jnp.transpose(jnp.broadcast_to(sums, (rows, 128)))[:1]


def project_qv_kernel(
    at_ref, norm_ref, w_ref, mask_ref, gain_ref, q_ref, v_ref, sq_ref, acc_ref
):
    step = pl.program_id(0)
    x_at = jnp.abs(at_ref[0] - step)
    parts, _, matrices, depth, cols = w_ref.shape
    rows = parts * depth
    weights = [w_ref[:, 0, m].reshape(rows, cols) for m in range(matrices)]
    pruned = masked(weights, mask_ref, (0, 2), x_at * (rows // BLK))
    part = jnp.dot(norm_ref[...], pruned, preferred_element_type=jnp.float32)

    @pl.when(step == 0)
    def _():
        acc_ref[...] = part

    @pl.when(step > 0)
    def _():
        total = acc_ref[...] + part
        query = total[:, :cols]
        q_ref[...] = query * gain_ref[...]
        v_ref[...] = total[:, cols:].astype(jnp.bfloat16)
        sq_ref[...] = row_sums(query)


def project_qv(at, normed, weights, masks, gain):
    rows, width = normed.shape
    parts, halves, matrices, depth, cols = weights.shape

    def fixed(*shape):
        return pl.BlockSpec(shape, lambda i, at: (0, 0))

    return pl.pallas_call(
        project_qv_kernel,
        grid_spec=pltpu.PrefetchScalarGridSpec(
            num_scalar_prefetch=1,
            grid=(halves,),
            in_specs=[
                pl.BlockSpec((rows, width // halves), lambda i, at: (0, jnp.abs(at[0] - i))),
                pl.BlockSpec((parts, 1, matrices, depth, cols), lambda i, at: (0, i, 0, 0, 0)),
                pl.BlockSpec(memory_space=pltpu.SMEM),
                fixed(1, cols),
            ],
            out_specs=[fixed(rows, cols), fixed(rows, cols), fixed(1, rows)],
            scratch_shapes=[pltpu.VMEM((rows, matrices * cols), jnp.float32)],
        ),
        out_shape=[
            jax.ShapeDtypeStruct((rows, cols), jnp.float32),
            jax.ShapeDtypeStruct((rows, cols), jnp.bfloat16),
            jax.ShapeDtypeStruct((1, rows), jnp.float32),
        ],
        compiler_params=pltpu.CompilerParams(vmem_limit_bytes=52 * MIB),
        name="project_qv",
    )(at, normed, weights, masks, gain)


def project_k_kernel(
    at_ref, norm_hbm, w00_ref, w01_ref, w10_ref, w11_ref, mask_ref, gain_ref, k_ref, sq_ref,
    norm_buf, w_buf, norm_sem,
):
    halves, half, _ = w_buf.shape
    depth = DEPTH
    chips = w00_ref.shape[0] // depth
    spots = [jnp.abs(at_ref[0] - i) for i in range(halves)]
    copies = []
    for i, x_at in enumerate(spots):
        columns = norm_hbm.at[:, pl.ds(pl.multiple_of(x_at * half, BLK), half)]
        copies.append(pltpu.make_async_copy(columns, norm_buf.at[i], norm_sem.at[i]))
        copies[i].start()
    for i, j, piece in ((0, 0, w00_ref), (0, 1, w01_ref), (1, 0, w10_ref), (1, 1, w11_ref)):
        core = jnp.abs(at_ref[1] - j)
        for z in range(chips):
            row = pl.multiple_of((z * 2 + core) * depth, 16)
            w_buf[i, pl.ds(row, depth), :] = piece[z * depth : (z + 1) * depth, :]
    total = None
    for i, x_at in enumerate(spots):
        copies[i].wait()
        pruned = masked([w_buf[i]], mask_ref, (1,), x_at * (half // BLK))
        part = jnp.dot(norm_buf[i], pruned, preferred_element_type=jnp.float32)
        total = part if total is None else total + part
    k_ref[...] = (total * gain_ref[...]).astype(jnp.bfloat16)
    sq_ref[...] = row_sums(total)


def project_k(at, normed, pieces, masks, gain):
    rows, width = normed.shape
    cols = pieces[0].shape[1]
    whole = pl.BlockSpec(memory_space=pltpu.VMEM)
    far = pl.BlockSpec(memory_space=pltpu.HBM)
    smem = pl.BlockSpec(memory_space=pltpu.SMEM)
    return pl.pallas_call(
        project_k_kernel,
        in_specs=[smem, far, whole, whole, whole, whole, smem, whole],
        out_specs=[whole, whole],
        out_shape=[
            jax.ShapeDtypeStruct((rows, cols), jnp.bfloat16),
            jax.ShapeDtypeStruct((1, rows), jnp.float32),
        ],
        scratch_shapes=[
            pltpu.VMEM((2, rows, width // 2), jnp.bfloat16),
            pltpu.VMEM((2, width // 2, cols), jnp.bfloat16),
            pltpu.SemaphoreType.DMA((2,)),
        ],
        compiler_params=pltpu.CompilerParams(vmem_limit_bytes=50 * MIB),
        name="project_k",
    )(at, normed, *pieces, masks, gain)


def attend_kernel(
    frame_ref, q_ref, k0_ref, k1_ref, k2_ref, v0_ref, v1_ref, v2_ref, totals_ref, out_ref
):
    rows, cols = q_ref.shape
    frame = frame_ref[0]
    ks, vs = (k0_ref, k1_ref, k2_ref), (v0_ref, v1_ref, v2_ref)
    scales = lax.rsqrt(totals_ref[...] * (1.0 / float(HEADS * HD)) + eps_rms)
    rq = jnp.transpose(jnp.broadcast_to(scales[3:4, :], (8, rows)))[:, :1]
    rks = scales * (HD**-0.5 * LOG2E)
    for h in range(cols // HD):
        span = slice(h * HD, (h + 1) * HD)
        query = (q_ref[:, span] * rq).astype(jnp.bfloat16)
        scores = []
        for back, key in enumerate(ks):
            dots = lax.dot_general(
                query, key[:, span], (((1,), (1,)), ((), ())), preferred_element_type=jnp.float32
            )
            scaled = dots * rks[back : back + 1, :]
            if back < 2:
                scaled = jnp.where(frame >= 2 - back, scaled, neg_large)
            scores.append(scaled)
        top = jnp.maximum(
            jnp.maximum(
                jnp.max(scores[0], axis=1, keepdims=True), jnp.max(scores[1], axis=1, keepdims=True)
            ),
            jnp.max(scores[2], axis=1, keepdims=True),
        )
        total = 0.0
        mixed = 0.0
        for s, value in zip(scores, vs):
            grown = jnp.exp2(s - top)
            total = total + jnp.sum(grown, axis=1, keepdims=True)
            mixed = mixed + jnp.dot(
                grown.astype(jnp.bfloat16), value[:, span], preferred_element_type=jnp.float32
            )
        out_ref[:, span] = (mixed / total).astype(jnp.bfloat16)


def attend(frame, q, ks, vs, totals):
    rows, cols = q.shape
    whole = pl.BlockSpec(memory_space=pltpu.VMEM)
    return pl.pallas_call(
        attend_kernel,
        in_specs=[pl.BlockSpec(memory_space=pltpu.SMEM)] + [whole] * 8,
        out_specs=whole,
        out_shape=jax.ShapeDtypeStruct((rows, cols), jnp.bfloat16),
        compiler_params=pltpu.CompilerParams(vmem_limit_bytes=28 * MIB),
        name="attend",
    )(frame, q, *ks, *vs, totals)


def passed_along(block, distance):
    devices = range(lax.axis_size("tm"))
    route = [(i - distance, i) for i in devices if i - distance in devices]
    return lax.ppermute(block, "tm", route)


def with_flipped(block, flip):
    size = lax.axis_size("tensor")
    return block + lax.ppermute(block, "tensor", [(i, i ^ flip) for i in range(size)])


def shards_on(mesh):
    xs, zs, cs = grid_of(mesh)
    everyone = [(x, z, c) for x in range(xs) for z in range(zs) for c in range(cs)]

    def tm(x, z, c):
        return (x * zs + z % zs) * cs + c

    x_swap = [(tm(x, z, c), tm(1 - x, z, c)) for x, z, c in everyone]
    core_swap = [(tm(x, z, c), tm(x, z, 1 - c)) for x, z, c in everyone]
    zc_groups = [[tm(x, z, c) for z in range(zs) for c in range(cs)] for x in range(xs)]
    z_groups = [[tm(x, z, c) for z in range(zs)] for x in range(xs) for c in range(cs)]

    def swapped(block, route):
        return lax.ppermute(block, "tm", route)

    def shards(
        tokens, shift_mod, scale_mod, w_query, w_key, w_value, prune_masks, query_gain, key_gain
    ):
        frame = lax.axis_index("tm")
        x_at = frame // (zs * cs)
        at = jnp.stack([x_at, frame % cs])
        both = jnp.concatenate(
            [w_query, w_value, swapped(w_query, x_swap), swapped(w_value, x_swap)], axis=0
        )
        weights = lax.all_gather(both, "tm", axis=0, tiled=True, axis_index_groups=zc_groups)
        weights = weights.reshape(zs * cs, xs, 2, *w_query.shape)

        own_k = lax.all_gather(w_key, "tm", axis=0, tiled=True, axis_index_groups=z_groups)
        across_k = swapped(own_k, x_swap)
        beside_k = swapped(own_k, core_swap)
        normed = modulate(tokens, shift_mod, scale_mod)
        across_k, normed = lax.optimization_barrier((across_k, normed))
        both_k = swapped(across_k, core_swap)
        keys, key_sum = project_k(
            at, normed, (own_k, beside_k, across_k, both_k), prune_masks, key_gain[None, :]
        )
        one_key, two_key = passed_along(keys, 1), passed_along(keys, 2)
        one_sum, two_sum = passed_along(key_sum, 1), passed_along(key_sum, 2)

        q, values, query_sum = project_qv(at, normed, weights, prune_masks, query_gain[None, :])
        query_sum, one_key, two_key, one_sum, two_sum = lax.optimization_barrier(
            (query_sum, one_key, two_key, one_sum, two_sum)
        )
        one_value = passed_along(values, 1)
        totals = with_flipped(jnp.concatenate([two_sum, one_sum, key_sum, query_sum]), 1)
        later_values, totals = lax.optimization_barrier((values, totals))
        two_value = passed_along(later_values, 2)
        flip = 2
        while flip < lax.axis_size("tensor"):
            totals = with_flipped(totals, flip)
            flip *= 2
        return attend(
            frame.reshape(1),
            q,
            (two_key, one_key, keys),
            (two_value, one_value, values),
            totals,
        )

    return shards


def solution(mesh):
    return jax.shard_map(
        shards_on(mesh),
        mesh=mesh,
        in_specs=(
            P("tm", None),
            P(),
            P(),
            P("tm", "tensor"),
            P("tm", "tensor"),
            P("tm", "tensor"),
            P(None, None, "tensor"),
            P("tensor"),
            P("tensor"),
        ),
        out_specs=P("tm", "tensor"),
        check_vma=False,
    )
```

```python
import jax
import jax.numpy as jnp
from jax import lax
from jax.experimental import pallas as pl
from jax.experimental.pallas import tpu as pltpu
from jax.sharding import PartitionSpec as P

HEADS = 24
HD = 128
BLK = 128
DEPTH = 80
LOG2E = 1.4426950408889634

eps_layer = 1e-06
eps_rms = 1e-06
neg_large = -1e30
MIB = 1024 * 1024


def grid_of(mesh):
    return 2, mesh.shape["tm"] // 4, 2


def norm_kernel(tok_ref, shift_ref, scale_ref, out_ref):
    values = tok_ref[...].astype(jnp.float32)
    width = values.shape[1]
    average = jnp.sum(values, axis=1, keepdims=True) * (1.0 / width)
    centred = values - average
    variance = jnp.sum(centred * centred, axis=1, keepdims=True) * (1.0 / width)
    normalized = centred * lax.rsqrt(variance + eps_layer)
    out_ref[...] = (normalized * (1.0 + scale_ref[...]) + shift_ref[...]).astype(jnp.bfloat16)


def modulate(tokens, shift_mod, scale_mod):
    rows, width = tokens.shape
    step = 64
    return pl.pallas_call(
        norm_kernel,
        grid=(rows // step,),
        in_specs=[
            pl.BlockSpec((step, width), lambda i: (i, 0)),
            pl.BlockSpec((1, width), lambda i: (0, 0)),
            pl.BlockSpec((1, width), lambda i: (0, 0)),
        ],
        out_specs=pl.BlockSpec((step, width), lambda i: (i, 0)),
        out_shape=jax.ShapeDtypeStruct((rows, width), jnp.bfloat16),
        compiler_params=pltpu.CompilerParams(vmem_limit_bytes=50 * MIB),
        name="modulate",
    )(tokens, shift_mod.reshape(1, width), scale_mod.reshape(1, width))


def masked(weight, mask_ref, matrices, first_block):
    rows, cols = weight.shape
    blocks = cols // BLK // len(matrices)
    pieces = []
    for r in range(rows // BLK):
        row = []
        for c in range(cols // BLK):
            kept = mask_ref[matrices[c // blocks], first_block + r, c % blocks] > 0
            block = weight[r * BLK : (r + 1) * BLK, c * BLK : (c + 1) * BLK]
            row.append(jnp.where(kept, block, jnp.zeros_like(block)))
        pieces.append(jnp.concatenate(row, axis=1))
    return jnp.concatenate(pieces, axis=0)


def row_sums(total):
    rows = total.shape[0]
    sums = jnp.sum(total * total, axis=1, keepdims=True)
    return jnp.transpose(jnp.broadcast_to(sums, (rows, 128)))[:1]


def project_qv_kernel(
    norm_ref, w_ref, mask_ref, gain_ref, q_ref, v_ref, sq_ref, acc_ref
):
    half = pl.program_id(0)
    parts, _, depth, cols = w_ref.shape
    rows = parts * depth
    weight = w_ref[...].reshape(rows, cols)
    pruned = masked(weight, mask_ref, (0, 2), half * (rows // BLK))
    part = jnp.dot(norm_ref[...], pruned, preferred_element_type=jnp.float32)

    @pl.when(half == 0)
    def _():
        acc_ref[...] = part

    @pl.when(half > 0)
    def _():
        total = acc_ref[...] + part
        query = total[:, : cols // 2]
        q_ref[...] = query * gain_ref[...]
        v_ref[...] = total[:, cols // 2 :].astype(jnp.bfloat16)
        sq_ref[...] = row_sums(query)


def project_qv(normed, weights, masks, gain):
    rows, width = normed.shape
    parts, halves, depth, cols2 = weights.shape
    cols = cols2 // 2

    def fixed(*shape):
        return pl.BlockSpec(shape, lambda i: (0, 0))

    return pl.pallas_call(
        project_qv_kernel,
        grid=(halves,),
        in_specs=[
            pl.BlockSpec((rows, width // halves), lambda i: (0, i)),
            pl.BlockSpec((parts, 1, depth, cols2), lambda i: (0, i, 0, 0)),
            pl.BlockSpec(memory_space=pltpu.SMEM),
            fixed(1, cols),
        ],
        out_specs=[fixed(rows, cols), fixed(rows, cols), fixed(1, rows)],
        out_shape=[
            jax.ShapeDtypeStruct((rows, cols), jnp.float32),
            jax.ShapeDtypeStruct((rows, cols), jnp.bfloat16),
            jax.ShapeDtypeStruct((1, rows), jnp.float32),
        ],
        scratch_shapes=[pltpu.VMEM((rows, cols2), jnp.float32)],
        compiler_params=pltpu.CompilerParams(vmem_limit_bytes=52 * MIB),
        name="project_qv",
    )(normed, weights, masks, gain)


def project_k_kernel(
    at_ref, norm_hbm, w00_ref, w01_ref, w10_ref, w11_ref, mask_ref, gain_ref, k_ref, sq_ref,
    norm_buf, w_buf, norm_sem,
):
    halves, half, _ = w_buf.shape
    depth = DEPTH
    chips = w00_ref.shape[0] // depth
    normed = pltpu.make_async_copy(norm_hbm, norm_buf, norm_sem)
    normed.start()
    for i, j, piece in ((0, 0, w00_ref), (0, 1, w01_ref), (1, 0, w10_ref), (1, 1, w11_ref)):
        core = jnp.abs(at_ref[1] - j)
        for z in range(chips):
            row = pl.multiple_of((z * 2 + core) * depth, 16)
            w_buf[i, pl.ds(row, depth), :] = piece[z * depth : (z + 1) * depth, :]
    normed.wait()
    total = None
    for i in range(halves):
        x_at = jnp.abs(at_ref[0] - i)
        pruned = masked(w_buf[i], mask_ref, (1,), x_at * (half // BLK))
        columns = pl.ds(pl.multiple_of(x_at * half, BLK), half)
        part = jnp.dot(norm_buf[:, columns], pruned, preferred_element_type=jnp.float32)
        total = part if total is None else total + part
    k_ref[...] = (total * gain_ref[...]).astype(jnp.bfloat16)
    sq_ref[...] = row_sums(total)


def project_k(at, normed, pieces, masks, gain):
    rows, width = normed.shape
    cols = pieces[0].shape[1]
    whole = pl.BlockSpec(memory_space=pltpu.VMEM)
    far = pl.BlockSpec(memory_space=pltpu.HBM)
    smem = pl.BlockSpec(memory_space=pltpu.SMEM)
    return pl.pallas_call(
        project_k_kernel,
        in_specs=[smem, far, whole, whole, whole, whole, smem, whole],
        out_specs=[whole, whole],
        out_shape=[
            jax.ShapeDtypeStruct((rows, cols), jnp.bfloat16),
            jax.ShapeDtypeStruct((1, rows), jnp.float32),
        ],
        scratch_shapes=[
            pltpu.VMEM((rows, width), jnp.bfloat16),
            pltpu.VMEM((2, width // 2, cols), jnp.bfloat16),
            pltpu.SemaphoreType.DMA,
        ],
        compiler_params=pltpu.CompilerParams(vmem_limit_bytes=50 * MIB),
        name="project_k",
    )(at, normed, *pieces, masks, gain)


def attend_kernel(
    frame_ref, q_ref, k0_ref, k1_ref, k2_ref, v0_ref, v1_ref, v2_ref, totals_ref, out_ref
):
    rows, cols = q_ref.shape
    frame = frame_ref[0]
    ks, vs = (k0_ref, k1_ref, k2_ref), (v0_ref, v1_ref, v2_ref)
    scales = lax.rsqrt(totals_ref[...] * (1.0 / float(HEADS * HD)) + eps_rms)
    rq = jnp.transpose(jnp.broadcast_to(scales[3:4, :], (8, rows)))[:, :1]
    rks = scales * (HD**-0.5 * LOG2E)
    for h in range(cols // HD):
        span = slice(h * HD, (h + 1) * HD)
        query = (q_ref[:, span] * rq).astype(jnp.bfloat16)
        scores = []
        for back, key in enumerate(ks):
            dots = lax.dot_general(
                query, key[:, span], (((1,), (1,)), ((), ())), preferred_element_type=jnp.float32
            )
            scaled = dots * rks[back : back + 1, :]
            if back < 2:
                scaled = jnp.where(frame >= 2 - back, scaled, neg_large)
            scores.append(scaled)
        top = jnp.maximum(
            jnp.maximum(
                jnp.max(scores[0], axis=1, keepdims=True), jnp.max(scores[1], axis=1, keepdims=True)
            ),
            jnp.max(scores[2], axis=1, keepdims=True),
        )
        total = 0.0
        mixed = 0.0
        for s, value in zip(scores, vs):
            grown = jnp.exp2(s - top)
            total = total + jnp.sum(grown, axis=1, keepdims=True)
            mixed = mixed + jnp.dot(
                grown.astype(jnp.bfloat16), value[:, span], preferred_element_type=jnp.float32
            )
        out_ref[:, span] = (mixed / total).astype(jnp.bfloat16)


def attend(frame, q, ks, vs, totals):
    rows, cols = q.shape
    whole = pl.BlockSpec(memory_space=pltpu.VMEM)
    return pl.pallas_call(
        attend_kernel,
        in_specs=[pl.BlockSpec(memory_space=pltpu.SMEM)] + [whole] * 8,
        out_specs=whole,
        out_shape=jax.ShapeDtypeStruct((rows, cols), jnp.bfloat16),
        compiler_params=pltpu.CompilerParams(vmem_limit_bytes=28 * MIB),
        name="attend",
    )(frame, q, *ks, *vs, totals)


def passed_along(block, distance):
    devices = range(lax.axis_size("tm"))
    route = [(i - distance, i) for i in devices if i - distance in devices]
    return lax.ppermute(block, "tm", route)


def with_flipped(block, flip):
    size = lax.axis_size("tensor")
    return block + lax.ppermute(block, "tensor", [(i, i ^ flip) for i in range(size)])


def shards_on(mesh):
    xs, zs, cs = grid_of(mesh)
    everyone = [(x, z, c) for x in range(xs) for z in range(zs) for c in range(cs)]

    def tm(x, z, c):
        return (x * zs + z % zs) * cs + c

    x_swap = [(tm(x, z, c), tm(1 - x, z, c)) for x, z, c in everyone]
    core_swap = [(tm(x, z, c), tm(x, z, 1 - c)) for x, z, c in everyone]
    zc_groups = [[tm(x, z, c) for z in range(zs) for c in range(cs)] for x in range(xs)]
    y_groups = [list(range(x, mesh.shape["tensor"], 2)) for x in range(2)]
    z_groups = [[tm(x, z, c) for z in range(zs)] for x in range(xs) for c in range(cs)]

    def swapped(block, route):
        return lax.ppermute(block, "tm", route)

    def shards(
        tokens, shift_mod, scale_mod, w_query, w_key, w_value, prune_masks, query_gain, key_gain
    ):
        frame = lax.axis_index("tm")
        x_at = frame // (zs * cs)
        mine = jnp.concatenate([w_query, w_value], axis=1)
        other = swapped(mine, x_swap)
        first = x_at == 0
        both = jnp.concatenate(
            [jnp.where(first, mine, other), jnp.where(first, other, mine)], axis=0
        )
        weights = lax.all_gather(both, "tm", axis=0, tiled=True, axis_index_groups=zc_groups)
        weights = weights.reshape(zs * cs, xs, mine.shape[0], mine.shape[1])

        own_k = lax.all_gather(w_key, "tm", axis=0, tiled=True, axis_index_groups=z_groups)
        across_k = swapped(own_k, x_swap)
        beside_k = swapped(own_k, core_swap)
        normed = modulate(tokens, shift_mod, scale_mod)
        across_k, normed = lax.optimization_barrier((across_k, normed))
        both_k = swapped(across_k, core_swap)
        at = jnp.stack([x_at, frame % cs])
        keys, key_sum = project_k(
            at, normed, (own_k, beside_k, across_k, both_k), prune_masks, key_gain[None, :]
        )
        one_key, two_key = passed_along(keys, 1), passed_along(keys, 2)
        one_sum, two_sum = passed_along(key_sum, 1), passed_along(key_sum, 2)

        q, values, query_sum = project_qv(normed, weights, prune_masks, query_gain[None, :])
        query_sum, one_key, two_key, one_sum, two_sum = lax.optimization_barrier(
            (query_sum, one_key, two_key, one_sum, two_sum)
        )
        two_value = passed_along(values, 2)
        totals = with_flipped(jnp.concatenate([two_sum, one_sum, key_sum, query_sum]), 1)
        later_values, totals = lax.optimization_barrier((values, totals))
        one_value = passed_along(later_values, 1)
        totals = lax.psum(totals, "tensor", axis_index_groups=y_groups)
        return attend(
            frame.reshape(1),
            q,
            (two_key, one_key, keys),
            (two_value, one_value, values),
            totals,
        )

    return shards


def solution(mesh):
    return jax.shard_map(
        shards_on(mesh),
        mesh=mesh,
        in_specs=(
            P("tm", None),
            P(),
            P(),
            P("tm", "tensor"),
            P("tm", "tensor"),
            P("tm", "tensor"),
            P(None, None, "tensor"),
            P("tensor"),
            P("tensor"),
        ),
        out_specs=P("tm", "tensor"),
        check_vma=False,
    )
```

```python
import jax
import jax.numpy as jnp
from jax import lax
from jax.experimental import pallas as pl
from jax.experimental.pallas import tpu as pltpu
from jax.sharding import PartitionSpec as P

HEADS = 24
HD = 128
BLK = 128
DEPTH = 80
LOG2E = 1.4426950408889634

eps_layer = 1e-06
eps_rms = 1e-06
neg_large = -1e30
MIB = 1024 * 1024


def grid_of(mesh):
    return 2, mesh.shape["tm"] // 4, 2


def norm_kernel(tok_ref, shift_ref, scale_ref, out_ref):
    values = tok_ref[...].astype(jnp.float32)
    width = values.shape[1]
    average = jnp.sum(values, axis=1, keepdims=True) * (1.0 / width)
    centred = values - average
    variance = jnp.sum(centred * centred, axis=1, keepdims=True) * (1.0 / width)
    normalized = centred * lax.rsqrt(variance + eps_layer)
    out_ref[...] = (normalized * (1.0 + scale_ref[...]) + shift_ref[...]).astype(jnp.bfloat16)


def modulate(tokens, shift_mod, scale_mod):
    rows, width = tokens.shape
    step = 64
    return pl.pallas_call(
        norm_kernel,
        grid=(rows // step,),
        in_specs=[
            pl.BlockSpec((step, width), lambda i: (i, 0)),
            pl.BlockSpec((1, width), lambda i: (0, 0)),
            pl.BlockSpec((1, width), lambda i: (0, 0)),
        ],
        out_specs=pl.BlockSpec((step, width), lambda i: (i, 0)),
        out_shape=jax.ShapeDtypeStruct((rows, width), jnp.bfloat16),
        compiler_params=pltpu.CompilerParams(vmem_limit_bytes=50 * MIB),
        name="modulate",
    )(tokens, shift_mod.reshape(1, width), scale_mod.reshape(1, width))


def masked(weight, mask_ref, matrices, first_block):
    rows, cols = weight.shape
    blocks = cols // BLK // len(matrices)
    pieces = []
    for r in range(rows // BLK):
        row = []
        for c in range(cols // BLK):
            kept = mask_ref[matrices[c // blocks], first_block + r, c % blocks] > 0
            block = weight[r * BLK : (r + 1) * BLK, c * BLK : (c + 1) * BLK]
            row.append(jnp.where(kept, block, jnp.zeros_like(block)))
        pieces.append(jnp.concatenate(row, axis=1))
    return jnp.concatenate(pieces, axis=0)


def row_sums(total):
    rows = total.shape[0]
    sums = jnp.sum(total * total, axis=1, keepdims=True)
    return jnp.transpose(jnp.broadcast_to(sums, (rows, 128)))[:1]


def project_qv_kernel(
    norm_ref, w_ref, mask_ref, gain_ref, q_ref, v_ref, sq_ref, acc_ref
):
    half = pl.program_id(0)
    parts, _, depth, cols = w_ref.shape
    rows = parts * depth
    weight = w_ref[...].reshape(rows, cols)
    pruned = masked(weight, mask_ref, (0, 2), half * (rows // BLK))
    part = jnp.dot(norm_ref[...], pruned, preferred_element_type=jnp.float32)

    @pl.when(half == 0)
    def _():
        acc_ref[...] = part

    @pl.when(half > 0)
    def _():
        total = acc_ref[...] + part
        query = total[:, : cols // 2]
        q_ref[...] = query * gain_ref[...]
        v_ref[...] = total[:, cols // 2 :].astype(jnp.bfloat16)
        sq_ref[...] = row_sums(query)


def project_qv(normed, weights, masks, gain):
    rows, width = normed.shape
    parts, halves, depth, cols2 = weights.shape
    cols = cols2 // 2

    def fixed(*shape):
        return pl.BlockSpec(shape, lambda i: (0, 0))

    return pl.pallas_call(
        project_qv_kernel,
        grid=(halves,),
        in_specs=[
            pl.BlockSpec((rows, width // halves), lambda i: (0, i)),
            pl.BlockSpec((parts, 1, depth, cols2), lambda i: (0, i, 0, 0)),
            pl.BlockSpec(memory_space=pltpu.SMEM),
            fixed(1, cols),
        ],
        out_specs=[fixed(rows, cols), fixed(rows, cols), fixed(1, rows)],
        out_shape=[
            jax.ShapeDtypeStruct((rows, cols), jnp.float32),
            jax.ShapeDtypeStruct((rows, cols), jnp.bfloat16),
            jax.ShapeDtypeStruct((1, rows), jnp.float32),
        ],
        scratch_shapes=[pltpu.VMEM((rows, cols2), jnp.float32)],
        compiler_params=pltpu.CompilerParams(vmem_limit_bytes=52 * MIB),
        name="project_qv",
    )(normed, weights, masks, gain)


def project_k_half(at_ref, step, norm_hbm, pieces, mask_ref, norm_buf, w_buf, norm_sem):
    half = w_buf.shape[0]
    depth = DEPTH
    x_at = jnp.abs(at_ref[0] - step)
    columns = norm_hbm.at[:, pl.ds(pl.multiple_of(x_at * half, BLK), half)]
    normed = pltpu.make_async_copy(columns, norm_buf, norm_sem)
    normed.start()
    for j, piece in enumerate(pieces):
        core = jnp.abs(at_ref[1] - j)
        for z in range(piece.shape[0] // depth):
            row = pl.multiple_of((z * 2 + core) * depth, 16)
            w_buf[pl.ds(row, depth), :] = piece[z * depth : (z + 1) * depth, :]
    pruned = masked(w_buf[...], mask_ref, (1,), x_at * (half // BLK))
    normed.wait()
    return jnp.dot(norm_buf[...], pruned, preferred_element_type=jnp.float32)


def project_k_first(at_ref, norm_hbm, mine_ref, beside_ref, mask_ref, part_ref, *scratch):
    part_ref[...] = project_k_half(at_ref, 0, norm_hbm, (mine_ref, beside_ref), mask_ref, *scratch)


def project_k_second(
    at_ref, norm_hbm, mine_ref, beside_ref, mask_ref, part_ref, gain_ref, k_ref, sq_ref, *scratch
):
    part = project_k_half(at_ref, 1, norm_hbm, (mine_ref, beside_ref), mask_ref, *scratch)
    total = part_ref[...] + part
    k_ref[...] = (total * gain_ref[...]).astype(jnp.bfloat16)
    sq_ref[...] = row_sums(total)


def project_k(at, normed, pieces, masks, part=None, gain=None):
    rows, width = normed.shape
    cols = pieces[0].shape[1]
    whole = pl.BlockSpec(memory_space=pltpu.VMEM)
    far = pl.BlockSpec(memory_space=pltpu.HBM)
    smem = pl.BlockSpec(memory_space=pltpu.SMEM)
    first = part is None
    return pl.pallas_call(
        project_k_first if first else project_k_second,
        in_specs=[smem, far, whole, whole, smem] + ([] if first else [whole, whole]),
        out_specs=whole if first else [whole, whole],
        out_shape=jax.ShapeDtypeStruct((rows, cols), jnp.float32)
        if first
        else [
            jax.ShapeDtypeStruct((rows, cols), jnp.bfloat16),
            jax.ShapeDtypeStruct((1, rows), jnp.float32),
        ],
        scratch_shapes=[
            pltpu.VMEM((rows, width // 2), jnp.bfloat16),
            pltpu.VMEM((width // 2, cols), jnp.bfloat16),
            pltpu.SemaphoreType.DMA,
        ],
        compiler_params=pltpu.CompilerParams(vmem_limit_bytes=50 * MIB),
        name="project_k_first" if first else "project_k_second",
    )(at, normed, *pieces, masks, *(() if first else (part, gain)))


def attend_kernel(
    frame_ref, q_ref, k0_ref, k1_ref, k2_ref, v0_ref, v1_ref, v2_ref, totals_ref, out_ref
):
    rows, cols = q_ref.shape
    frame = frame_ref[0]
    ks, vs = (k0_ref, k1_ref, k2_ref), (v0_ref, v1_ref, v2_ref)
    scales = lax.rsqrt(totals_ref[...] * (1.0 / float(HEADS * HD)) + eps_rms)
    rq = jnp.transpose(jnp.broadcast_to(scales[3:4, :], (8, rows)))[:, :1]
    rks = scales * (HD**-0.5 * LOG2E)
    for h in range(cols // HD):
        span = slice(h * HD, (h + 1) * HD)
        query = (q_ref[:, span] * rq).astype(jnp.bfloat16)
        scores = []
        for back, key in enumerate(ks):
            dots = lax.dot_general(
                query, key[:, span], (((1,), (1,)), ((), ())), preferred_element_type=jnp.float32
            )
            scaled = dots * rks[back : back + 1, :]
            if back < 2:
                scaled = jnp.where(frame >= 2 - back, scaled, neg_large)
            scores.append(scaled)
        top = jnp.maximum(
            jnp.maximum(
                jnp.max(scores[0], axis=1, keepdims=True), jnp.max(scores[1], axis=1, keepdims=True)
            ),
            jnp.max(scores[2], axis=1, keepdims=True),
        )
        total = 0.0
        mixed = 0.0
        for s, value in zip(scores, vs):
            grown = jnp.exp2(s - top)
            total = total + jnp.sum(grown, axis=1, keepdims=True)
            mixed = mixed + jnp.dot(
                grown.astype(jnp.bfloat16), value[:, span], preferred_element_type=jnp.float32
            )
        out_ref[:, span] = (mixed / total).astype(jnp.bfloat16)


def attend(frame, q, ks, vs, totals):
    rows, cols = q.shape
    whole = pl.BlockSpec(memory_space=pltpu.VMEM)
    return pl.pallas_call(
        attend_kernel,
        in_specs=[pl.BlockSpec(memory_space=pltpu.SMEM)] + [whole] * 8,
        out_specs=whole,
        out_shape=jax.ShapeDtypeStruct((rows, cols), jnp.bfloat16),
        compiler_params=pltpu.CompilerParams(vmem_limit_bytes=28 * MIB),
        name="attend",
    )(frame, q, *ks, *vs, totals)


def passed_along(block, distance):
    devices = range(lax.axis_size("tm"))
    route = [(i - distance, i) for i in devices if i - distance in devices]
    return lax.ppermute(block, "tm", route)


def with_flipped(block, flip):
    size = lax.axis_size("tensor")
    return block + lax.ppermute(block, "tensor", [(i, i ^ flip) for i in range(size)])


def shards_on(mesh):
    xs, zs, cs = grid_of(mesh)
    everyone = [(x, z, c) for x in range(xs) for z in range(zs) for c in range(cs)]

    def tm(x, z, c):
        return (x * zs + z % zs) * cs + c

    x_swap = [(tm(x, z, c), tm(1 - x, z, c)) for x, z, c in everyone]
    core_swap = [(tm(x, z, c), tm(x, z, 1 - c)) for x, z, c in everyone]
    zc_groups = [[tm(x, z, c) for z in range(zs) for c in range(cs)] for x in range(xs)]
    y_groups = [list(range(x, mesh.shape["tensor"], 2)) for x in range(2)]
    z_groups = [[tm(x, z, c) for z in range(zs)] for x in range(xs) for c in range(cs)]

    def swapped(block, route):
        return lax.ppermute(block, "tm", route)

    def shards(
        tokens, shift_mod, scale_mod, w_query, w_key, w_value, prune_masks, query_gain, key_gain
    ):
        frame = lax.axis_index("tm")
        x_at = frame // (zs * cs)
        rows, cols = w_query.shape
        mine = jnp.pad(w_query, ((0, 0), (0, cols))) + jnp.pad(w_value, ((0, 0), (cols, 0)))
        other = swapped(mine, x_swap)
        first = x_at == 0
        upper, lower = jnp.where(first, mine, other), jnp.where(first, other, mine)
        both = jnp.pad(upper, ((0, rows), (0, 0))) + jnp.pad(lower, ((rows, 0), (0, 0)))
        weights = lax.all_gather(both, "tm", axis=0, tiled=True, axis_index_groups=zc_groups)
        weights = weights.reshape(zs * cs, xs, mine.shape[0], mine.shape[1])

        own_k = lax.all_gather(w_key, "tm", axis=0, tiled=True, axis_index_groups=z_groups)
        across_k = swapped(own_k, x_swap)
        beside_k = swapped(own_k, core_swap)
        normed = modulate(tokens, shift_mod, scale_mod)
        across_k, normed = lax.optimization_barrier((across_k, normed))
        both_k = swapped(across_k, core_swap)
        at = jnp.stack([x_at, frame % cs])
        part = project_k(at, normed, (own_k, beside_k), prune_masks)
        both_k, part = lax.optimization_barrier((both_k, part))
        keys, key_sum = project_k(
            at, normed, (across_k, both_k), prune_masks, part, key_gain[None, :]
        )
        one_key, two_key = passed_along(keys, 1), passed_along(keys, 2)
        one_sum, two_sum = passed_along(key_sum, 1), passed_along(key_sum, 2)

        q, values, query_sum = project_qv(normed, weights, prune_masks, query_gain[None, :])
        query_sum, one_key, two_key, one_sum, two_sum = lax.optimization_barrier(
            (query_sum, one_key, two_key, one_sum, two_sum)
        )
        two_value = passed_along(values, 2)
        totals = with_flipped(jnp.concatenate([two_sum, one_sum, key_sum, query_sum]), 1)
        later_values, totals = lax.optimization_barrier((values, totals))
        one_value = passed_along(later_values, 1)
        totals = lax.psum(totals, "tensor", axis_index_groups=y_groups)
        return attend(
            frame.reshape(1),
            q,
            (two_key, one_key, keys),
            (two_value, one_value, values),
            totals,
        )

    return shards


def solution(mesh):
    return jax.shard_map(
        shards_on(mesh),
        mesh=mesh,
        in_specs=(
            P("tm", None),
            P(),
            P(),
            P("tm", "tensor"),
            P("tm", "tensor"),
            P("tm", "tensor"),
            P(None, None, "tensor"),
            P("tensor"),
            P("tensor"),
        ),
        out_specs=P("tm", "tensor"),
        check_vma=False,
    )
```

```python
import jax
import jax.numpy as jnp
from jax import lax
from jax.experimental import pallas as pl
from jax.experimental.pallas import tpu as pltpu
from jax.sharding import PartitionSpec as P

HEADS = 24
HD = 128
BLK = 128
DEPTH = 80
BLOCK_ROWS = 40
LOG2E = 1.4426950408889634

eps_layer = 1e-06
eps_rms = 1e-06
neg_large = -1e30
MIB = 1024 * 1024


def grid_of(mesh):
    return 2, mesh.shape["tm"] // 4, 2


def norm_kernel(tok_ref, shift_ref, scale_ref, out_ref):
    values = tok_ref[...].astype(jnp.float32)
    width = values.shape[1]
    average = jnp.sum(values, axis=1, keepdims=True) * (1.0 / width)
    centred = values - average
    variance = jnp.sum(centred * centred, axis=1, keepdims=True) * (1.0 / width)
    normalized = centred * lax.rsqrt(variance + eps_layer)
    out_ref[...] = (normalized * (1.0 + scale_ref[...]) + shift_ref[...]).astype(jnp.bfloat16)


def modulate(tokens, shift_mod, scale_mod):
    rows, width = tokens.shape
    step = 64
    return pl.pallas_call(
        norm_kernel,
        grid=(rows // step,),
        in_specs=[
            pl.BlockSpec((step, width), lambda i: (i, 0)),
            pl.BlockSpec((1, width), lambda i: (0, 0)),
            pl.BlockSpec((1, width), lambda i: (0, 0)),
        ],
        out_specs=pl.BlockSpec((step, width), lambda i: (i, 0)),
        out_shape=jax.ShapeDtypeStruct((rows, width), jnp.bfloat16),
        compiler_params=pltpu.CompilerParams(vmem_limit_bytes=56 * MIB),
        name="modulate",
    )(tokens, shift_mod.reshape(1, width), scale_mod.reshape(1, width))


def masked(weight, mask_ref, matrices, first_block):
    rows, cols = weight.shape
    blocks = cols // BLK // len(matrices)
    pieces = []
    for r in range(rows // BLK):
        row = []
        for c in range(cols // BLK):
            block_row = matrices[c // blocks] * BLOCK_ROWS + first_block + r
            kept = mask_ref[block_row * blocks + c % blocks] > 0
            block = weight[r * BLK : (r + 1) * BLK, c * BLK : (c + 1) * BLK]
            row.append(jnp.where(kept, block, jnp.zeros_like(block)))
        pieces.append(jnp.concatenate(row, axis=1))
    return jnp.concatenate(pieces, axis=0)


def row_sums(total):
    rows = total.shape[0]
    sums = jnp.sum(total * total, axis=1, keepdims=True)
    return jnp.transpose(jnp.broadcast_to(sums, (rows, 128)))[:1]


def project_qv_kernel(
    norm_ref, w_ref, mask_ref, gain_ref, q_ref, v_ref, sq_ref, acc_ref
):
    half = pl.program_id(0)
    parts, _, depth, cols = w_ref.shape
    rows = parts * depth
    weight = w_ref[...].reshape(rows, cols)
    pruned = masked(weight, mask_ref, (0, 2), half * (rows // BLK))
    part = jnp.dot(norm_ref[...], pruned, preferred_element_type=jnp.float32)

    @pl.when(half == 0)
    def _():
        acc_ref[...] = part

    @pl.when(half > 0)
    def _():
        total = acc_ref[...] + part
        query = total[:, : cols // 2]
        q_ref[...] = query * gain_ref[...]
        v_ref[...] = total[:, cols // 2 :].astype(jnp.bfloat16)
        sq_ref[...] = row_sums(query)


def project_qv(normed, weights, masks, gain):
    rows, width = normed.shape
    parts, halves, depth, cols2 = weights.shape
    cols = cols2 // 2

    def fixed(*shape):
        return pl.BlockSpec(shape, lambda i: (0, 0))

    return pl.pallas_call(
        project_qv_kernel,
        grid=(halves,),
        in_specs=[
            pl.BlockSpec((rows, width // halves), lambda i: (0, i)),
            pl.BlockSpec((parts, 1, depth, cols2), lambda i: (0, i, 0, 0)),
            pl.BlockSpec(memory_space=pltpu.SMEM),
            fixed(1, cols),
        ],
        out_specs=[fixed(rows, cols), fixed(rows, cols), fixed(1, rows)],
        out_shape=[
            jax.ShapeDtypeStruct((rows, cols), jnp.float32),
            jax.ShapeDtypeStruct((rows, cols), jnp.bfloat16),
            jax.ShapeDtypeStruct((1, rows), jnp.float32),
        ],
        scratch_shapes=[pltpu.VMEM((rows, cols2), jnp.float32)],
        compiler_params=pltpu.CompilerParams(vmem_limit_bytes=52 * MIB),
        name="project_qv",
    )(normed, weights, masks, gain)


def project_k_half(at_ref, step, norm_hbm, pieces, mask_ref, norm_buf, w_buf, norm_sem):
    half = w_buf.shape[0]
    depth = DEPTH
    x_at = jnp.abs(at_ref[0] - step)
    columns = norm_hbm.at[:, pl.ds(pl.multiple_of(x_at * half, BLK), half)]
    normed = pltpu.make_async_copy(columns, norm_buf, norm_sem)
    normed.start()
    for j, piece in enumerate(pieces):
        core = jnp.abs(at_ref[1] - j)
        for z in range(piece.shape[0] // depth):
            row = pl.multiple_of((z * 2 + core) * depth, 16)
            w_buf[pl.ds(row, depth), :] = piece[z * depth : (z + 1) * depth, :]
    pruned = masked(w_buf[...], mask_ref, (1,), x_at * (half // BLK))
    normed.wait()
    return jnp.dot(norm_buf[...], pruned, preferred_element_type=jnp.float32)


def project_k_first(at_ref, norm_hbm, mine_ref, beside_ref, mask_ref, part_ref, *scratch):
    part_ref[...] = project_k_half(at_ref, 0, norm_hbm, (mine_ref, beside_ref), mask_ref, *scratch)


def project_k_second(
    at_ref, norm_hbm, mine_ref, beside_ref, mask_ref, part_ref, gain_ref, k_ref, sq_ref, *scratch
):
    part = project_k_half(at_ref, 1, norm_hbm, (mine_ref, beside_ref), mask_ref, *scratch)
    total = part_ref[...] + part
    k_ref[...] = (total * gain_ref[...]).astype(jnp.bfloat16)
    sq_ref[...] = row_sums(total)


def project_k(at, normed, pieces, masks, part=None, gain=None):
    rows, width = normed.shape
    cols = pieces[0].shape[1]
    whole = pl.BlockSpec(memory_space=pltpu.VMEM)
    far = pl.BlockSpec(memory_space=pltpu.HBM)
    smem = pl.BlockSpec(memory_space=pltpu.SMEM)
    first = part is None
    return pl.pallas_call(
        project_k_first if first else project_k_second,
        in_specs=[smem, far, whole, whole, smem] + ([] if first else [whole, whole]),
        out_specs=whole if first else [whole, whole],
        out_shape=jax.ShapeDtypeStruct((rows, cols), jnp.float32)
        if first
        else [
            jax.ShapeDtypeStruct((rows, cols), jnp.bfloat16),
            jax.ShapeDtypeStruct((1, rows), jnp.float32),
        ],
        scratch_shapes=[
            pltpu.VMEM((rows, width // 2), jnp.bfloat16),
            pltpu.VMEM((width // 2, cols), jnp.bfloat16),
            pltpu.SemaphoreType.DMA,
        ],
        compiler_params=pltpu.CompilerParams(vmem_limit_bytes=50 * MIB),
        name="project_k_first" if first else "project_k_second",
    )(at, normed, *pieces, masks, *(() if first else (part, gain)))


def attend_kernel(
    frame_ref, q_ref, k0_ref, k1_ref, k2_ref, v0_ref, v1_ref, v2_ref, totals_ref, out_ref
):
    rows, cols = q_ref.shape
    frame = frame_ref[0]
    ks, vs = (k0_ref, k1_ref, k2_ref), (v0_ref, v1_ref, v2_ref)
    scales = lax.rsqrt(totals_ref[...] * (1.0 / float(HEADS * HD)) + eps_rms)
    rq = jnp.transpose(jnp.broadcast_to(scales[3:4, :], (8, rows)))[:, :1]
    rks = scales * (HD**-0.5 * LOG2E)
    for h in range(cols // HD):
        span = slice(h * HD, (h + 1) * HD)
        query = (q_ref[:, span] * rq).astype(jnp.bfloat16)
        scores = []
        for back, key in enumerate(ks):
            dots = lax.dot_general(
                query, key[:, span], (((1,), (1,)), ((), ())), preferred_element_type=jnp.float32
            )
            scaled = dots * rks[back : back + 1, :]
            if back < 2:
                scaled = jnp.where(frame >= 2 - back, scaled, neg_large)
            scores.append(scaled)
        top = jnp.maximum(
            jnp.maximum(
                jnp.max(scores[0], axis=1, keepdims=True), jnp.max(scores[1], axis=1, keepdims=True)
            ),
            jnp.max(scores[2], axis=1, keepdims=True),
        )
        total = 0.0
        mixed = 0.0
        for s, value in zip(scores, vs):
            grown = jnp.exp2(s - top)
            total = total + jnp.sum(grown, axis=1, keepdims=True)
            mixed = mixed + jnp.dot(
                grown.astype(jnp.bfloat16), value[:, span], preferred_element_type=jnp.float32
            )
        out_ref[:, span] = (mixed / total).astype(jnp.bfloat16)


def attend(frame, q, ks, vs, totals):
    rows, cols = q.shape
    whole = pl.BlockSpec(memory_space=pltpu.VMEM)
    return pl.pallas_call(
        attend_kernel,
        in_specs=[pl.BlockSpec(memory_space=pltpu.SMEM)] + [whole] * 8,
        out_specs=whole,
        out_shape=jax.ShapeDtypeStruct((rows, cols), jnp.bfloat16),
        compiler_params=pltpu.CompilerParams(vmem_limit_bytes=28 * MIB),
        name="attend",
    )(frame, q, *ks, *vs, totals)


def passed_along(block, distance):
    devices = range(lax.axis_size("tm"))
    route = [(i - distance, i) for i in devices if i - distance in devices]
    return lax.ppermute(block, "tm", route)


def with_flipped(block, flip):
    size = lax.axis_size("tensor")
    return block + lax.ppermute(block, "tensor", [(i, i ^ flip) for i in range(size)])


def shards_on(mesh):
    xs, zs, cs = grid_of(mesh)
    everyone = [(x, z, c) for x in range(xs) for z in range(zs) for c in range(cs)]

    def tm(x, z, c):
        return (x * zs + z % zs) * cs + c

    x_swap = [(tm(x, z, c), tm(1 - x, z, c)) for x, z, c in everyone]
    core_swap = [(tm(x, z, c), tm(x, z, 1 - c)) for x, z, c in everyone]
    zc_groups = [[tm(x, z, c) for z in range(zs) for c in range(cs)] for x in range(xs)]
    y_groups = [list(range(x, mesh.shape["tensor"], 2)) for x in range(2)]
    z_groups = [[tm(x, z, c) for z in range(zs)] for x in range(xs) for c in range(cs)]

    def swapped(block, route):
        return lax.ppermute(block, "tm", route)

    def shards(
        tokens, shift_mod, scale_mod, w_query, w_key, w_value, prune_masks, query_gain, key_gain
    ):
        frame = lax.axis_index("tm")
        x_at = frame // (zs * cs)
        rows, cols = w_query.shape
        mine = jnp.pad(w_query, ((0, 0), (0, cols))) + jnp.pad(w_value, ((0, 0), (cols, 0)))
        small = (
            jnp.stack([x_at, frame % cs]),
            prune_masks.reshape(-1),
            query_gain[None, :],
            key_gain[None, :],
        )
        other, small = lax.optimization_barrier((swapped(mine, x_swap), small))
        at, masks, query_gain, key_gain = small
        first = x_at == 0
        upper, lower = jnp.where(first, mine, other), jnp.where(first, other, mine)
        both = jnp.pad(upper, ((0, rows), (0, 0))) + jnp.pad(lower, ((rows, 0), (0, 0)))
        weights = lax.all_gather(both, "tm", axis=0, tiled=True, axis_index_groups=zc_groups)
        weights = weights.reshape(zs * cs, xs, mine.shape[0], mine.shape[1])

        own_k = lax.all_gather(w_key, "tm", axis=0, tiled=True, axis_index_groups=z_groups)
        across_k = swapped(own_k, x_swap)
        beside_k = swapped(own_k, core_swap)
        normed = modulate(tokens, shift_mod, scale_mod)
        across_k, normed = lax.optimization_barrier((across_k, normed))
        both_k = swapped(across_k, core_swap)
        part = project_k(at, normed, (own_k, beside_k), masks)
        both_k, part = lax.optimization_barrier((both_k, part))
        keys, key_sum = project_k(at, normed, (across_k, both_k), masks, part, key_gain)
        one_key, two_key = passed_along(keys, 1), passed_along(keys, 2)
        one_sum, two_sum = passed_along(key_sum, 1), passed_along(key_sum, 2)

        q, values, query_sum = project_qv(normed, weights, masks, query_gain)
        query_sum, one_key, two_key, one_sum, two_sum = lax.optimization_barrier(
            (query_sum, one_key, two_key, one_sum, two_sum)
        )
        two_value = passed_along(values, 2)
        totals = with_flipped(jnp.concatenate([two_sum, one_sum, key_sum, query_sum]), 1)
        later_values, totals = lax.optimization_barrier((values, totals))
        one_value = passed_along(later_values, 1)
        totals = lax.psum(totals, "tensor", axis_index_groups=y_groups)
        return attend(
            frame.reshape(1),
            q,
            (two_key, one_key, keys),
            (two_value, one_value, values),
            totals,
        )

    return shards


def solution(mesh):
    return jax.shard_map(
        shards_on(mesh),
        mesh=mesh,
        in_specs=(
            P("tm", None),
            P(),
            P(),
            P("tm", "tensor"),
            P("tm", "tensor"),
            P("tm", "tensor"),
            P(None, None, "tensor"),
            P("tensor"),
            P("tensor"),
        ),
        out_specs=P("tm", "tensor"),
        check_vma=False,
    )
```

```python
import jax
import jax.numpy as jnp
from jax import lax
from jax.experimental import pallas as pl
from jax.experimental.pallas import tpu as pltpu
from jax.sharding import PartitionSpec as P

HEADS = 24
HD = 128
BLK = 128
DEPTH = 80
BLOCK_ROWS = 40
LOG2E = 1.4426950408889634

eps_layer = 1e-06
eps_rms = 1e-06
neg_large = -1e30
MIB = 1024 * 1024


def grid_of(mesh):
    return 2, mesh.shape["tm"] // 4, 2


def norm_kernel(tok_ref, shift_ref, scale_ref, out_ref):
    values = tok_ref[...].astype(jnp.float32)
    width = values.shape[1]
    average = jnp.sum(values, axis=1, keepdims=True) * (1.0 / width)
    centred = values - average
    variance = jnp.sum(centred * centred, axis=1, keepdims=True) * (1.0 / width)
    normalized = centred * lax.rsqrt(variance + eps_layer)
    out_ref[...] = (normalized * (1.0 + scale_ref[...]) + shift_ref[...]).astype(jnp.bfloat16)


def modulate(tokens, shift_mod, scale_mod):
    rows, width = tokens.shape
    step = 64
    return pl.pallas_call(
        norm_kernel,
        grid=(rows // step,),
        in_specs=[
            pl.BlockSpec((step, width), lambda i: (i, 0)),
            pl.BlockSpec((1, width), lambda i: (0, 0)),
            pl.BlockSpec((1, width), lambda i: (0, 0)),
        ],
        out_specs=pl.BlockSpec((step, width), lambda i: (i, 0)),
        out_shape=jax.ShapeDtypeStruct((rows, width), jnp.bfloat16),
        compiler_params=pltpu.CompilerParams(vmem_limit_bytes=56 * MIB),
        name="modulate",
    )(tokens, shift_mod.reshape(1, width), scale_mod.reshape(1, width))


def masked(weight, mask_ref, matrices, first_block):
    rows, cols = weight.shape
    blocks = cols // BLK // len(matrices)
    pieces = []
    for r in range(rows // BLK):
        row = []
        for c in range(cols // BLK):
            block_row = matrices[c // blocks] * BLOCK_ROWS + first_block + r
            kept = mask_ref[block_row * blocks + c % blocks] > 0
            block = weight[r * BLK : (r + 1) * BLK, c * BLK : (c + 1) * BLK]
            row.append(jnp.where(kept, block, jnp.zeros_like(block)))
        pieces.append(jnp.concatenate(row, axis=1))
    return jnp.concatenate(pieces, axis=0)


def row_sums(total):
    rows = total.shape[0]
    sums = jnp.sum(total * total, axis=1, keepdims=True)
    return jnp.transpose(jnp.broadcast_to(sums, (rows, 128)))[:1]


def project_qv_kernel(
    norm_ref, w_ref, mask_ref, gain_ref, q_ref, v_ref, sq_ref, acc_ref
):
    half = pl.program_id(0)
    parts, _, depth, cols = w_ref.shape
    rows = parts * depth
    weight = w_ref[...].reshape(rows, cols)
    pruned = masked(weight, mask_ref, (0, 2), half * (rows // BLK))
    part = jnp.dot(norm_ref[...], pruned, preferred_element_type=jnp.float32)

    @pl.when(half == 0)
    def _():
        acc_ref[...] = part

    @pl.when(half > 0)
    def _():
        total = acc_ref[...] + part
        query = total[:, : cols // 2]
        q_ref[...] = query * gain_ref[...]
        v_ref[...] = total[:, cols // 2 :].astype(jnp.bfloat16)
        sq_ref[...] = row_sums(query)


def project_qv(normed, weights, masks, gain):
    rows, width = normed.shape
    parts, halves, depth, cols2 = weights.shape
    cols = cols2 // 2

    def fixed(*shape):
        return pl.BlockSpec(shape, lambda i: (0, 0))

    return pl.pallas_call(
        project_qv_kernel,
        grid=(halves,),
        in_specs=[
            pl.BlockSpec((rows, width // halves), lambda i: (0, i)),
            pl.BlockSpec((parts, 1, depth, cols2), lambda i: (0, i, 0, 0)),
            pl.BlockSpec(memory_space=pltpu.SMEM),
            fixed(1, cols),
        ],
        out_specs=[fixed(rows, cols), fixed(rows, cols), fixed(1, rows)],
        out_shape=[
            jax.ShapeDtypeStruct((rows, cols), jnp.float32),
            jax.ShapeDtypeStruct((rows, cols), jnp.bfloat16),
            jax.ShapeDtypeStruct((1, rows), jnp.float32),
        ],
        scratch_shapes=[pltpu.VMEM((rows, cols2), jnp.float32)],
        compiler_params=pltpu.CompilerParams(vmem_limit_bytes=52 * MIB),
        name="project_qv",
    )(normed, weights, masks, gain)


def project_k_half(at_ref, step, norm_hbm, pieces, mask_ref, norm_buf, w_buf, norm_sem):
    half = w_buf.shape[0]
    depth = DEPTH
    x_at = jnp.abs(at_ref[0] - step)
    columns = norm_hbm.at[:, pl.ds(pl.multiple_of(x_at * half, BLK), half)]
    normed = pltpu.make_async_copy(columns, norm_buf, norm_sem)
    normed.start()
    for j, piece in enumerate(pieces):
        core = jnp.abs(at_ref[1] - j)
        for z in range(piece.shape[0] // depth):
            row = pl.multiple_of((z * 2 + core) * depth, 16)
            w_buf[pl.ds(row, depth), :] = piece[z * depth : (z + 1) * depth, :]
    pruned = masked(w_buf[...], mask_ref, (1,), x_at * (half // BLK))
    normed.wait()
    return jnp.dot(norm_buf[...], pruned, preferred_element_type=jnp.float32)


def project_k_first(at_ref, norm_hbm, mine_ref, beside_ref, mask_ref, part_ref, *scratch):
    part_ref[...] = project_k_half(at_ref, 0, norm_hbm, (mine_ref, beside_ref), mask_ref, *scratch)


def project_k_second(
    at_ref, norm_hbm, mine_ref, beside_ref, mask_ref, part_ref, gain_ref, k_ref, sq_ref, *scratch
):
    part = project_k_half(at_ref, 1, norm_hbm, (mine_ref, beside_ref), mask_ref, *scratch)
    total = part_ref[...] + part
    k_ref[...] = (total * gain_ref[...]).astype(jnp.bfloat16)
    sq_ref[...] = row_sums(total)


def project_k(at, normed, pieces, masks, part=None, gain=None):
    rows, width = normed.shape
    cols = pieces[0].shape[1]
    whole = pl.BlockSpec(memory_space=pltpu.VMEM)
    far = pl.BlockSpec(memory_space=pltpu.HBM)
    smem = pl.BlockSpec(memory_space=pltpu.SMEM)
    first = part is None
    return pl.pallas_call(
        project_k_first if first else project_k_second,
        in_specs=[smem, far, whole, whole, smem] + ([] if first else [whole, whole]),
        out_specs=whole if first else [whole, whole],
        out_shape=jax.ShapeDtypeStruct((rows, cols), jnp.float32)
        if first
        else [
            jax.ShapeDtypeStruct((rows, cols), jnp.bfloat16),
            jax.ShapeDtypeStruct((1, rows), jnp.float32),
        ],
        scratch_shapes=[
            pltpu.VMEM((rows, width // 2), jnp.bfloat16),
            pltpu.VMEM((width // 2, cols), jnp.bfloat16),
            pltpu.SemaphoreType.DMA,
        ],
        compiler_params=pltpu.CompilerParams(vmem_limit_bytes=50 * MIB),
        name="project_k_first" if first else "project_k_second",
    )(at, normed, *pieces, masks, *(() if first else (part, gain)))


def attend_kernel(
    frame_ref, q_ref, k0_ref, k1_ref, k2_ref, v0_ref, v1_ref, v2_ref, totals_ref, out_ref
):
    rows, cols = q_ref.shape
    frame = frame_ref[0]
    ks, vs = (k0_ref, k1_ref, k2_ref), (v0_ref, v1_ref, v2_ref)
    scales = lax.rsqrt(totals_ref[...] * (1.0 / float(HEADS * HD)) + eps_rms)
    rq = jnp.transpose(jnp.broadcast_to(scales[3:4, :], (8, rows)))[:, :1]
    rks = scales * (HD**-0.5 * LOG2E)
    for h in range(cols // HD):
        span = slice(h * HD, (h + 1) * HD)
        query = (q_ref[:, span] * rq).astype(jnp.bfloat16)
        scores = []
        for back, key in enumerate(ks):
            dots = lax.dot_general(
                query, key[:, span], (((1,), (1,)), ((), ())), preferred_element_type=jnp.float32
            )
            scaled = dots * rks[back : back + 1, :]
            if back < 2:
                scaled = jnp.where(frame >= 2 - back, scaled, neg_large)
            scores.append(scaled)
        top = jnp.maximum(
            jnp.maximum(
                jnp.max(scores[0], axis=1, keepdims=True), jnp.max(scores[1], axis=1, keepdims=True)
            ),
            jnp.max(scores[2], axis=1, keepdims=True),
        )
        total = 0.0
        mixed = 0.0
        for s, value in zip(scores, vs):
            grown = jnp.exp2(s - top)
            total = total + jnp.sum(grown, axis=1, keepdims=True)
            mixed = mixed + jnp.dot(
                grown.astype(jnp.bfloat16), value[:, span], preferred_element_type=jnp.float32
            )
        out_ref[:, span] = (mixed / total).astype(jnp.bfloat16)


def attend(frame, q, ks, vs, totals):
    rows, cols = q.shape
    whole = pl.BlockSpec(memory_space=pltpu.VMEM)
    return pl.pallas_call(
        attend_kernel,
        in_specs=[pl.BlockSpec(memory_space=pltpu.SMEM)] + [whole] * 8,
        out_specs=whole,
        out_shape=jax.ShapeDtypeStruct((rows, cols), jnp.bfloat16),
        compiler_params=pltpu.CompilerParams(vmem_limit_bytes=28 * MIB),
        name="attend",
    )(frame, q, *ks, *vs, totals)


def passed_along(block, distance):
    devices = range(lax.axis_size("tm"))
    route = [(i - distance, i) for i in devices if i - distance in devices]
    return lax.ppermute(block, "tm", route)


def with_flipped(block, flip):
    size = lax.axis_size("tensor")
    return block + lax.ppermute(block, "tensor", [(i, i ^ flip) for i in range(size)])


def shards_on(mesh):
    xs, zs, cs = grid_of(mesh)
    everyone = [(x, z, c) for x in range(xs) for z in range(zs) for c in range(cs)]

    def tm(x, z, c):
        return (x * zs + z % zs) * cs + c

    x_swap = [(tm(x, z, c), tm(1 - x, z, c)) for x, z, c in everyone]
    core_swap = [(tm(x, z, c), tm(x, z, 1 - c)) for x, z, c in everyone]
    zc_groups = [[tm(x, z, c) for z in range(zs) for c in range(cs)] for x in range(xs)]
    y_groups = [list(range(x, mesh.shape["tensor"], 2)) for x in range(2)]
    z_groups = [[tm(x, z, c) for z in range(zs)] for x in range(xs) for c in range(cs)]

    def swapped(block, route):
        return lax.ppermute(block, "tm", route)

    def shards(
        tokens, shift_mod, scale_mod, w_query, w_key, w_value, prune_masks, query_gain, key_gain
    ):
        frame = lax.axis_index("tm")
        x_at = frame // (zs * cs)
        rows, cols = w_query.shape
        mine = jnp.pad(w_query, ((0, 0), (0, cols))) + jnp.pad(w_value, ((0, 0), (cols, 0)))
        small = (
            jnp.stack([x_at, frame % cs]),
            prune_masks.reshape(-1),
            query_gain[None, :],
            key_gain[None, :],
        )
        other, small = lax.optimization_barrier((swapped(mine, x_swap), small))
        at, masks, query_gain, key_gain = small
        first = x_at == 0
        above, below = ((0, rows), (0, 0)), ((rows, 0), (0, 0))
        both = jnp.where(
            first,
            jnp.pad(mine, above) + jnp.pad(other, below),
            jnp.pad(other, above) + jnp.pad(mine, below),
        )
        weights = lax.all_gather(both, "tm", axis=0, tiled=True, axis_index_groups=zc_groups)
        weights = weights.reshape(zs * cs, xs, mine.shape[0], mine.shape[1])

        own_k = lax.all_gather(w_key, "tm", axis=0, tiled=True, axis_index_groups=z_groups)
        across_k = swapped(own_k, x_swap)
        beside_k = swapped(own_k, core_swap)
        normed = modulate(tokens, shift_mod, scale_mod)
        across_k, normed = lax.optimization_barrier((across_k, normed))
        both_k = swapped(across_k, core_swap)
        part = project_k(at, normed, (own_k, beside_k), masks)
        both_k, part = lax.optimization_barrier((both_k, part))
        keys, key_sum = project_k(at, normed, (across_k, both_k), masks, part, key_gain)
        one_key, two_key = passed_along(keys, 1), passed_along(keys, 2)
        one_sum, two_sum = passed_along(key_sum, 1), passed_along(key_sum, 2)

        q, values, query_sum = project_qv(normed, weights, masks, query_gain)
        query_sum, one_key, two_key, one_sum, two_sum = lax.optimization_barrier(
            (query_sum, one_key, two_key, one_sum, two_sum)
        )
        two_value = passed_along(values, 2)
        totals = with_flipped(jnp.concatenate([two_sum, one_sum, key_sum, query_sum]), 1)
        later_values, totals = lax.optimization_barrier((values, totals))
        one_value = passed_along(later_values, 1)
        totals = lax.psum(totals, "tensor", axis_index_groups=y_groups)
        return attend(
            frame.reshape(1),
            q,
            (two_key, one_key, keys),
            (two_value, one_value, values),
            totals,
        )

    return shards


def solution(mesh):
    return jax.shard_map(
        shards_on(mesh),
        mesh=mesh,
        in_specs=(
            P("tm", None),
            P(),
            P(),
            P("tm", "tensor"),
            P("tm", "tensor"),
            P("tm", "tensor"),
            P(None, None, "tensor"),
            P("tensor"),
            P("tensor"),
        ),
        out_specs=P("tm", "tensor"),
        check_vma=False,
    )
```

```python
import jax
import jax.numpy as jnp
from jax import lax
from jax.experimental import pallas as pl
from jax.experimental.pallas import tpu as pltpu
from jax.sharding import PartitionSpec as P

HEADS = 24
HD = 128
BLK = 128
DEPTH = 80
BLOCK_ROWS = 40
LOG2E = 1.4426950408889634

eps_layer = 1e-06
eps_rms = 1e-06
neg_large = -1e30
MIB = 1024 * 1024


def grid_of(mesh):
    return 2, mesh.shape["tm"] // 4, 2


def norm_kernel(tok_ref, shift_ref, scale_ref, out_ref):
    values = tok_ref[...].astype(jnp.float32)
    width = values.shape[1]
    average = jnp.sum(values, axis=1, keepdims=True) * (1.0 / width)
    centred = values - average
    variance = jnp.sum(centred * centred, axis=1, keepdims=True) * (1.0 / width)
    normalized = centred * lax.rsqrt(variance + eps_layer)
    out_ref[...] = (normalized * (1.0 + scale_ref[...]) + shift_ref[...]).astype(jnp.bfloat16)


def modulate(tokens, shift_mod, scale_mod):
    rows, width = tokens.shape
    step = 64
    return pl.pallas_call(
        norm_kernel,
        grid=(rows // step,),
        in_specs=[
            pl.BlockSpec((step, width), lambda i: (i, 0)),
            pl.BlockSpec((1, width), lambda i: (0, 0)),
            pl.BlockSpec((1, width), lambda i: (0, 0)),
        ],
        out_specs=pl.BlockSpec((step, width), lambda i: (i, 0)),
        out_shape=jax.ShapeDtypeStruct((rows, width), jnp.bfloat16),
        compiler_params=pltpu.CompilerParams(vmem_limit_bytes=56 * MIB),
        name="modulate",
    )(tokens, shift_mod.reshape(1, width), scale_mod.reshape(1, width))


def masked(weight, mask_ref, matrices, first_block):
    rows, cols = weight.shape
    blocks = cols // BLK // len(matrices)
    pieces = []
    for r in range(rows // BLK):
        row = []
        for c in range(cols // BLK):
            block_row = matrices[c // blocks] * BLOCK_ROWS + first_block + r
            kept = mask_ref[block_row * blocks + c % blocks] > 0
            block = weight[r * BLK : (r + 1) * BLK, c * BLK : (c + 1) * BLK]
            row.append(jnp.where(kept, block, jnp.zeros_like(block)))
        pieces.append(jnp.concatenate(row, axis=1))
    return jnp.concatenate(pieces, axis=0)


def row_sums(total):
    rows = total.shape[0]
    sums = jnp.sum(total * total, axis=1, keepdims=True)
    return jnp.transpose(jnp.broadcast_to(sums, (rows, 128)))[:1]


def project_qv_kernel(
    norm_ref, w_ref, mask_ref, gain_ref, q_ref, v_ref, sq_ref, acc_ref
):
    half = pl.program_id(0)
    parts, _, depth, cols = w_ref.shape
    rows = parts * depth
    weight = w_ref[...].reshape(rows, cols)
    pruned = masked(weight, mask_ref, (0, 2), half * (rows // BLK))
    part = jnp.dot(norm_ref[...], pruned, preferred_element_type=jnp.float32)

    @pl.when(half == 0)
    def _():
        acc_ref[...] = part

    @pl.when(half > 0)
    def _():
        total = acc_ref[...] + part
        query = total[:, : cols // 2]
        q_ref[...] = query * gain_ref[...]
        v_ref[...] = total[:, cols // 2 :].astype(jnp.bfloat16)
        sq_ref[...] = row_sums(query)


def project_qv(normed, weights, masks, gain):
    rows, width = normed.shape
    parts, halves, depth, cols2 = weights.shape
    cols = cols2 // 2

    def fixed(*shape):
        return pl.BlockSpec(shape, lambda i: (0, 0))

    return pl.pallas_call(
        project_qv_kernel,
        grid=(halves,),
        in_specs=[
            pl.BlockSpec((rows, width // halves), lambda i: (0, i)),
            pl.BlockSpec((parts, 1, depth, cols2), lambda i: (0, i, 0, 0)),
            pl.BlockSpec(memory_space=pltpu.SMEM),
            fixed(1, cols),
        ],
        out_specs=[fixed(rows, cols), fixed(rows, cols), fixed(1, rows)],
        out_shape=[
            jax.ShapeDtypeStruct((rows, cols), jnp.float32),
            jax.ShapeDtypeStruct((rows, cols), jnp.bfloat16),
            jax.ShapeDtypeStruct((1, rows), jnp.float32),
        ],
        scratch_shapes=[pltpu.VMEM((rows, cols2), jnp.float32)],
        compiler_params=pltpu.CompilerParams(vmem_limit_bytes=52 * MIB),
        name="project_qv",
    )(normed, weights, masks, gain)


def project_k_half(at_ref, step, norm_hbm, pieces, mask_ref, norm_buf, w_buf, norm_sem):
    half = w_buf.shape[0]
    depth = DEPTH
    x_at = jnp.abs(at_ref[0] - step)
    columns = norm_hbm.at[:, pl.ds(pl.multiple_of(x_at * half, BLK), half)]
    normed = pltpu.make_async_copy(columns, norm_buf, norm_sem)
    normed.start()
    for j, piece in enumerate(pieces):
        core = jnp.abs(at_ref[1] - j)
        for z in range(piece.shape[0] // depth):
            row = pl.multiple_of((z * 2 + core) * depth, 16)
            w_buf[pl.ds(row, depth), :] = piece[z * depth : (z + 1) * depth, :]
    pruned = masked(w_buf[...], mask_ref, (1,), x_at * (half // BLK))
    normed.wait()
    return jnp.dot(norm_buf[...], pruned, preferred_element_type=jnp.float32)


def project_k_first(at_ref, norm_hbm, mine_ref, beside_ref, mask_ref, part_ref, *scratch):
    part_ref[...] = project_k_half(at_ref, 0, norm_hbm, (mine_ref, beside_ref), mask_ref, *scratch)


def project_k_second(
    at_ref, norm_hbm, mine_ref, beside_ref, mask_ref, part_ref, gain_ref, k_ref, sq_ref, *scratch
):
    part = project_k_half(at_ref, 1, norm_hbm, (mine_ref, beside_ref), mask_ref, *scratch)
    total = part_ref[...] + part
    k_ref[...] = (total * gain_ref[...]).astype(jnp.bfloat16)
    sq_ref[...] = row_sums(total)


def project_k(at, normed, pieces, masks, part=None, gain=None):
    rows, width = normed.shape
    cols = pieces[0].shape[1]
    whole = pl.BlockSpec(memory_space=pltpu.VMEM)
    far = pl.BlockSpec(memory_space=pltpu.HBM)
    smem = pl.BlockSpec(memory_space=pltpu.SMEM)
    first = part is None
    return pl.pallas_call(
        project_k_first if first else project_k_second,
        in_specs=[smem, far, whole, whole, smem] + ([] if first else [whole, whole]),
        out_specs=whole if first else [whole, whole],
        out_shape=jax.ShapeDtypeStruct((rows, cols), jnp.float32)
        if first
        else [
            jax.ShapeDtypeStruct((rows, cols), jnp.bfloat16),
            jax.ShapeDtypeStruct((1, rows), jnp.float32),
        ],
        scratch_shapes=[
            pltpu.VMEM((rows, width // 2), jnp.bfloat16),
            pltpu.VMEM((width // 2, cols), jnp.bfloat16),
            pltpu.SemaphoreType.DMA,
        ],
        compiler_params=pltpu.CompilerParams(vmem_limit_bytes=50 * MIB),
        name="project_k_first" if first else "project_k_second",
    )(at, normed, *pieces, masks, *(() if first else (part, gain)))


def attend_kernel(
    frame_ref, q_ref, k0_ref, k1_ref, k2_ref, v0_ref, v1_ref, v2_ref, totals_ref, out_ref
):
    rows, cols = q_ref.shape
    frame = frame_ref[0]
    ks, vs = (k0_ref, k1_ref, k2_ref), (v0_ref, v1_ref, v2_ref)
    scales = lax.rsqrt(totals_ref[...] * (1.0 / float(HEADS * HD)) + eps_rms)
    rq = jnp.transpose(jnp.broadcast_to(scales[3:4, :], (8, rows)))[:, :1]
    rks = scales * (HD**-0.5 * LOG2E)
    for h in range(cols // HD):
        span = slice(h * HD, (h + 1) * HD)
        query = (q_ref[:, span] * rq).astype(jnp.bfloat16)
        scores = []
        for back, key in enumerate(ks):
            dots = lax.dot_general(
                query, key[:, span], (((1,), (1,)), ((), ())), preferred_element_type=jnp.float32
            )
            scaled = dots * rks[back : back + 1, :]
            if back < 2:
                scaled = jnp.where(frame >= 2 - back, scaled, neg_large)
            scores.append(scaled)
        top = jnp.maximum(
            jnp.maximum(
                jnp.max(scores[0], axis=1, keepdims=True), jnp.max(scores[1], axis=1, keepdims=True)
            ),
            jnp.max(scores[2], axis=1, keepdims=True),
        )
        total = 0.0
        mixed = 0.0
        for s, value in zip(scores, vs):
            grown = jnp.exp2(s - top)
            total = total + jnp.sum(grown, axis=1, keepdims=True)
            mixed = mixed + jnp.dot(
                grown.astype(jnp.bfloat16), value[:, span], preferred_element_type=jnp.float32
            )
        out_ref[:, span] = (mixed / total).astype(jnp.bfloat16)


def attend(frame, q, ks, vs, totals):
    rows, cols = q.shape
    whole = pl.BlockSpec(memory_space=pltpu.VMEM)
    return pl.pallas_call(
        attend_kernel,
        in_specs=[pl.BlockSpec(memory_space=pltpu.SMEM)] + [whole] * 8,
        out_specs=whole,
        out_shape=jax.ShapeDtypeStruct((rows, cols), jnp.bfloat16),
        compiler_params=pltpu.CompilerParams(vmem_limit_bytes=28 * MIB),
        name="attend",
    )(frame, q, *ks, *vs, totals)


def passed_along(block, distance):
    devices = range(lax.axis_size("tm"))
    route = [(i - distance, i) for i in devices if i - distance in devices]
    return lax.ppermute(block, "tm", route)


def with_flipped(block, flip):
    size = lax.axis_size("tensor")
    return block + lax.ppermute(block, "tensor", [(i, i ^ flip) for i in range(size)])


def shards_on(mesh):
    xs, zs, cs = grid_of(mesh)
    everyone = [(x, z, c) for x in range(xs) for z in range(zs) for c in range(cs)]

    def tm(x, z, c):
        return (x * zs + z % zs) * cs + c

    x_swap = [(tm(x, z, c), tm(1 - x, z, c)) for x, z, c in everyone]
    core_swap = [(tm(x, z, c), tm(x, z, 1 - c)) for x, z, c in everyone]
    zc_groups = [[tm(x, z, c) for z in range(zs) for c in range(cs)] for x in range(xs)]
    y_groups = [list(range(x, mesh.shape["tensor"], 2)) for x in range(2)]
    z_groups = [[tm(x, z, c) for z in range(zs)] for x in range(xs) for c in range(cs)]

    def swapped(block, route):
        return lax.ppermute(block, "tm", route)

    def shards(
        tokens, shift_mod, scale_mod, w_query, w_key, w_value, prune_masks, query_gain, key_gain
    ):
        frame = lax.axis_index("tm")
        x_at = frame // (zs * cs)
        rows, cols = w_query.shape
        mine = jnp.pad(w_query, ((0, 0), (0, cols))) + jnp.pad(w_value, ((0, 0), (cols, 0)))
        small = (
            jnp.stack([x_at, frame % cs]),
            prune_masks.reshape(-1),
            query_gain[None, :],
            key_gain[None, :],
        )
        other, small = lax.optimization_barrier((swapped(mine, x_swap), small))
        at, masks, query_gain, key_gain = small
        first = x_at == 0
        above, below = ((0, rows), (0, 0)), ((rows, 0), (0, 0))
        both = jnp.where(
            first,
            jnp.pad(mine, above) + jnp.pad(other, below),
            jnp.pad(other, above) + jnp.pad(mine, below),
        )
        weights = lax.all_gather(both, "tm", axis=0, tiled=True, axis_index_groups=zc_groups)
        weights = weights.reshape(zs * cs, xs, mine.shape[0], mine.shape[1])

        own_k = lax.all_gather(w_key, "tm", axis=0, tiled=True, axis_index_groups=z_groups)
        across_k = swapped(own_k, x_swap)
        beside_k = swapped(own_k, core_swap)
        normed = modulate(tokens, shift_mod, scale_mod)
        across_k, normed = lax.optimization_barrier((across_k, normed))
        both_k = swapped(across_k, core_swap)
        part = project_k(at, normed, (own_k, beside_k), masks)
        both_k, part = lax.optimization_barrier((both_k, part))
        keys, key_sum = project_k(at, normed, (across_k, both_k), masks, part, key_gain)
        one_key, two_key = passed_along(keys, 1), passed_along(keys, 2)
        one_sum, two_sum = passed_along(key_sum, 1), passed_along(key_sum, 2)

        q, values, query_sum = project_qv(normed, weights, masks, query_gain)
        query_sum, one_key, two_key, one_sum, two_sum = lax.optimization_barrier(
            (query_sum, one_key, two_key, one_sum, two_sum)
        )
        two_value = passed_along(values, 2)
        totals = with_flipped(jnp.concatenate([two_sum, one_sum, key_sum, query_sum]), 1)
        one_value = passed_along(values, 1)
        totals = lax.psum(totals, "tensor", axis_index_groups=y_groups)
        return attend(
            frame.reshape(1),
            q,
            (two_key, one_key, keys),
            (two_value, one_value, values),
            totals,
        )

    return shards


def solution(mesh):
    return jax.shard_map(
        shards_on(mesh),
        mesh=mesh,
        in_specs=(
            P("tm", None),
            P(),
            P(),
            P("tm", "tensor"),
            P("tm", "tensor"),
            P("tm", "tensor"),
            P(None, None, "tensor"),
            P("tensor"),
            P("tensor"),
        ),
        out_specs=P("tm", "tensor"),
        check_vma=False,
    )
```

```python
import jax
import jax.numpy as jnp
from jax import lax
from jax.experimental import pallas as pl
from jax.experimental.pallas import tpu as pltpu
from jax.sharding import PartitionSpec as P

HEADS = 24
HD = 128
BLK = 128
DEPTH = 80
BLOCK_ROWS = 40
LOG2E = 1.4426950408889634

eps_layer = 1e-06
eps_rms = 1e-06
neg_large = -1e30
MIB = 1024 * 1024


def grid_of(mesh):
    return 2, mesh.shape["tm"] // 4, 2


def norm_kernel(tok_ref, shift_ref, scale_ref, out_ref):
    values = tok_ref[...].astype(jnp.float32)
    width = values.shape[1]
    average = jnp.sum(values, axis=1, keepdims=True) * (1.0 / width)
    centred = values - average
    variance = jnp.sum(centred * centred, axis=1, keepdims=True) * (1.0 / width)
    normalized = centred * lax.rsqrt(variance + eps_layer)
    out_ref[...] = (normalized * (1.0 + scale_ref[...]) + shift_ref[...]).astype(jnp.bfloat16)


def modulate(tokens, shift_mod, scale_mod):
    rows, width = tokens.shape
    step = 64
    return pl.pallas_call(
        norm_kernel,
        grid=(rows // step,),
        in_specs=[
            pl.BlockSpec((step, width), lambda i: (i, 0)),
            pl.BlockSpec((1, width), lambda i: (0, 0)),
            pl.BlockSpec((1, width), lambda i: (0, 0)),
        ],
        out_specs=pl.BlockSpec((step, width), lambda i: (i, 0)),
        out_shape=jax.ShapeDtypeStruct((rows, width), jnp.bfloat16),
        compiler_params=pltpu.CompilerParams(vmem_limit_bytes=56 * MIB),
        name="modulate",
    )(tokens, shift_mod.reshape(1, width), scale_mod.reshape(1, width))


def masked(weight, mask_ref, matrices, first_block):
    rows, cols = weight.shape
    blocks = cols // BLK // len(matrices)
    pieces = []
    for r in range(rows // BLK):
        row = []
        for c in range(cols // BLK):
            block_row = matrices[c // blocks] * BLOCK_ROWS + first_block + r
            kept = mask_ref[block_row * blocks + c % blocks] > 0
            block = weight[r * BLK : (r + 1) * BLK, c * BLK : (c + 1) * BLK]
            row.append(jnp.where(kept, block, jnp.zeros_like(block)))
        pieces.append(jnp.concatenate(row, axis=1))
    return jnp.concatenate(pieces, axis=0)


def row_sums(total):
    rows = total.shape[0]
    sums = jnp.sum(total * total, axis=1, keepdims=True)
    return jnp.transpose(jnp.broadcast_to(sums, (rows, 128)))[:1]


def project_qv_kernel(
    norm_ref, w_ref, mask_ref, gain_ref, q_ref, v_ref, sq_ref, acc_ref
):
    half = pl.program_id(0)
    parts, _, depth, cols = w_ref.shape
    rows = parts * depth
    weight = w_ref[...].reshape(rows, cols)
    pruned = masked(weight, mask_ref, (0, 2), half * (rows // BLK))
    part = jnp.dot(norm_ref[...], pruned, preferred_element_type=jnp.float32)

    @pl.when(half == 0)
    def _():
        acc_ref[...] = part

    @pl.when(half > 0)
    def _():
        total = acc_ref[...] + part
        query = total[:, : cols // 2]
        q_ref[...] = query * gain_ref[...]
        v_ref[...] = total[:, cols // 2 :].astype(jnp.bfloat16)
        sq_ref[...] = row_sums(query)


def project_qv(normed, weights, masks, gain):
    rows, width = normed.shape
    parts, halves, depth, cols2 = weights.shape
    cols = cols2 // 2

    def fixed(*shape):
        return pl.BlockSpec(shape, lambda i: (0, 0))

    return pl.pallas_call(
        project_qv_kernel,
        grid=(halves,),
        in_specs=[
            pl.BlockSpec((rows, width // halves), lambda i: (0, i)),
            pl.BlockSpec((parts, 1, depth, cols2), lambda i: (0, i, 0, 0)),
            pl.BlockSpec(memory_space=pltpu.SMEM),
            fixed(1, cols),
        ],
        out_specs=[fixed(rows, cols), fixed(rows, cols), fixed(1, rows)],
        out_shape=[
            jax.ShapeDtypeStruct((rows, cols), jnp.float32),
            jax.ShapeDtypeStruct((rows, cols), jnp.bfloat16),
            jax.ShapeDtypeStruct((1, rows), jnp.float32),
        ],
        scratch_shapes=[pltpu.VMEM((rows, cols2), jnp.float32)],
        compiler_params=pltpu.CompilerParams(vmem_limit_bytes=52 * MIB),
        name="project_qv",
    )(normed, weights, masks, gain)


def project_k_half(at_ref, step, norm_hbm, pieces, mask_ref, norm_buf, w_buf, norm_sem):
    half = w_buf.shape[0]
    depth = DEPTH
    x_at = jnp.abs(at_ref[0] - step)
    columns = norm_hbm.at[:, pl.ds(pl.multiple_of(x_at * half, BLK), half)]
    normed = pltpu.make_async_copy(columns, norm_buf, norm_sem)
    normed.start()
    for j, piece in enumerate(pieces):
        core = jnp.abs(at_ref[1] - j)
        for z in range(piece.shape[0] // depth):
            row = pl.multiple_of((z * 2 + core) * depth, 16)
            w_buf[pl.ds(row, depth), :] = piece[z * depth : (z + 1) * depth, :]
    pruned = masked(w_buf[...], mask_ref, (1,), x_at * (half // BLK))
    normed.wait()
    return jnp.dot(norm_buf[...], pruned, preferred_element_type=jnp.float32)


def project_k_first(at_ref, norm_hbm, mine_ref, beside_ref, mask_ref, part_ref, *scratch):
    part_ref[...] = project_k_half(at_ref, 0, norm_hbm, (mine_ref, beside_ref), mask_ref, *scratch)


def project_k_second(
    at_ref, norm_hbm, mine_ref, beside_ref, mask_ref, part_ref, gain_ref, k_ref, sq_ref, *scratch
):
    part = project_k_half(at_ref, 1, norm_hbm, (mine_ref, beside_ref), mask_ref, *scratch)
    total = part_ref[...] + part
    k_ref[...] = (total * gain_ref[...]).astype(jnp.bfloat16)
    sq_ref[...] = row_sums(total)


def project_k(at, normed, pieces, masks, part=None, gain=None):
    rows, width = normed.shape
    cols = pieces[0].shape[1]
    whole = pl.BlockSpec(memory_space=pltpu.VMEM)
    far = pl.BlockSpec(memory_space=pltpu.HBM)
    smem = pl.BlockSpec(memory_space=pltpu.SMEM)
    first = part is None
    return pl.pallas_call(
        project_k_first if first else project_k_second,
        in_specs=[smem, far, whole, whole, smem] + ([] if first else [whole, whole]),
        out_specs=whole if first else [whole, whole],
        out_shape=jax.ShapeDtypeStruct((rows, cols), jnp.float32)
        if first
        else [
            jax.ShapeDtypeStruct((rows, cols), jnp.bfloat16),
            jax.ShapeDtypeStruct((1, rows), jnp.float32),
        ],
        scratch_shapes=[
            pltpu.VMEM((rows, width // 2), jnp.bfloat16),
            pltpu.VMEM((width // 2, cols), jnp.bfloat16),
            pltpu.SemaphoreType.DMA,
        ],
        compiler_params=pltpu.CompilerParams(vmem_limit_bytes=50 * MIB),
        name="project_k_first" if first else "project_k_second",
    )(at, normed, *pieces, masks, *(() if first else (part, gain)))


def attend_kernel(
    frame_ref, q_ref, k0_ref, k1_ref, k2_ref, v0_ref, v1_ref, v2_ref, totals_ref, out_ref
):
    rows, cols = q_ref.shape
    frame = frame_ref[0]
    ks, vs = (k0_ref, k1_ref, k2_ref), (v0_ref, v1_ref, v2_ref)
    scales = lax.rsqrt(totals_ref[...] * (1.0 / float(HEADS * HD)) + eps_rms)
    rq = jnp.transpose(jnp.broadcast_to(scales[3:4, :], (8, rows)))[:, :1]
    rks = scales * (HD**-0.5 * LOG2E)
    for h in range(cols // HD):
        span = slice(h * HD, (h + 1) * HD)
        query = (q_ref[:, span] * rq).astype(jnp.bfloat16)
        scores = []
        for back, key in enumerate(ks):
            dots = lax.dot_general(
                query, key[:, span], (((1,), (1,)), ((), ())), preferred_element_type=jnp.float32
            )
            scaled = dots * rks[back : back + 1, :]
            if back < 2:
                scaled = jnp.where(frame >= 2 - back, scaled, neg_large)
            scores.append(scaled)
        top = jnp.maximum(
            jnp.maximum(
                jnp.max(scores[0], axis=1, keepdims=True), jnp.max(scores[1], axis=1, keepdims=True)
            ),
            jnp.max(scores[2], axis=1, keepdims=True),
        )
        total = 0.0
        mixed = 0.0
        for s, value in zip(scores, vs):
            grown = jnp.exp2(s - top)
            total = total + jnp.sum(grown, axis=1, keepdims=True)
            mixed = mixed + jnp.dot(
                grown.astype(jnp.bfloat16), value[:, span], preferred_element_type=jnp.float32
            )
        out_ref[:, span] = (mixed / total).astype(jnp.bfloat16)


def attend(frame, q, ks, vs, totals):
    rows, cols = q.shape
    whole = pl.BlockSpec(memory_space=pltpu.VMEM)
    return pl.pallas_call(
        attend_kernel,
        in_specs=[pl.BlockSpec(memory_space=pltpu.SMEM)] + [whole] * 8,
        out_specs=whole,
        out_shape=jax.ShapeDtypeStruct((rows, cols), jnp.bfloat16),
        compiler_params=pltpu.CompilerParams(vmem_limit_bytes=28 * MIB),
        name="attend",
    )(frame, q, *ks, *vs, totals)


def passed_along(block, distance):
    devices = range(lax.axis_size("tm"))
    route = [(i - distance, i) for i in devices if i - distance in devices]
    return lax.ppermute(block, "tm", route)


def shards_on(mesh):
    xs, zs, cs = grid_of(mesh)
    everyone = [(x, z, c) for x in range(xs) for z in range(zs) for c in range(cs)]

    def tm(x, z, c):
        return (x * zs + z % zs) * cs + c

    x_swap = [(tm(x, z, c), tm(1 - x, z, c)) for x, z, c in everyone]
    core_swap = [(tm(x, z, c), tm(x, z, 1 - c)) for x, z, c in everyone]
    zc_groups = [[tm(x, z, c) for z in range(zs) for c in range(cs)] for x in range(xs)]
    y_groups = [list(range(x, mesh.shape["tensor"], 2)) for x in range(2)]
    z_groups = [[tm(x, z, c) for z in range(zs)] for x in range(xs) for c in range(cs)]

    def swapped(block, route):
        return lax.ppermute(block, "tm", route)

    def shards(
        tokens, shift_mod, scale_mod, w_query, w_key, w_value, prune_masks, query_gain, key_gain
    ):
        frame = lax.axis_index("tm")
        x_at = frame // (zs * cs)
        rows, cols = w_query.shape
        mine = jnp.pad(w_query, ((0, 0), (0, cols))) + jnp.pad(w_value, ((0, 0), (cols, 0)))
        small = (
            jnp.stack([x_at, frame % cs]),
            prune_masks.reshape(-1),
            query_gain[None, :],
            key_gain[None, :],
        )
        other, small = lax.optimization_barrier((swapped(mine, x_swap), small))
        at, masks, query_gain, key_gain = small
        first = x_at == 0
        above, below = ((0, rows), (0, 0)), ((rows, 0), (0, 0))
        both = jnp.where(
            first,
            jnp.pad(mine, above) + jnp.pad(other, below),
            jnp.pad(other, above) + jnp.pad(mine, below),
        )
        weights = lax.all_gather(both, "tm", axis=0, tiled=True, axis_index_groups=zc_groups)
        weights = weights.reshape(zs * cs, xs, mine.shape[0], mine.shape[1])

        own_k = lax.all_gather(w_key, "tm", axis=0, tiled=True, axis_index_groups=z_groups)
        across_k = swapped(own_k, x_swap)
        beside_k = swapped(own_k, core_swap)
        normed = modulate(tokens, shift_mod, scale_mod)
        across_k, normed = lax.optimization_barrier((across_k, normed))
        both_k = swapped(across_k, core_swap)
        part = project_k(at, normed, (own_k, beside_k), masks)
        both_k, part = lax.optimization_barrier((both_k, part))
        keys, key_sum = project_k(at, normed, (across_k, both_k), masks, part, key_gain)
        one_key, two_key = passed_along(keys, 1), passed_along(keys, 2)
        one_sum, two_sum = passed_along(key_sum, 1), passed_along(key_sum, 2)

        q, values, query_sum = project_qv(normed, weights, masks, query_gain)
        query_sum, one_key, two_key, one_sum, two_sum = lax.optimization_barrier(
            (query_sum, one_key, two_key, one_sum, two_sum)
        )
        two_value = passed_along(values, 2)
        sums = jnp.concatenate([two_sum, one_sum, key_sum, query_sum])
        size = lax.axis_size("tensor")
        share = lax.ppermute(sums, "tensor", [(i, i ^ 1) for i in range(size)])
        later_values, share = lax.optimization_barrier((values, share))
        one_value = passed_along(later_values, 1)
        totals = sums + share
        totals = lax.psum(totals, "tensor", axis_index_groups=y_groups)
        return attend(
            frame.reshape(1),
            q,
            (two_key, one_key, keys),
            (two_value, one_value, values),
            totals,
        )

    return shards


def solution(mesh):
    return jax.shard_map(
        shards_on(mesh),
        mesh=mesh,
        in_specs=(
            P("tm", None),
            P(),
            P(),
            P("tm", "tensor"),
            P("tm", "tensor"),
            P("tm", "tensor"),
            P(None, None, "tensor"),
            P("tensor"),
            P("tensor"),
        ),
        out_specs=P("tm", "tensor"),
        check_vma=False,
    )
```
